512 devices in a mesh: gx: 16 (over z_hi, x, core), gy: 32 (over y, z_lo).
Axes of the slice: x: 4, y: 8, z: 8 (z_hi: 2, z_lo: 4; z = z_hi * 4 + z_lo), core: 2. Of those that a mesh axis runs over, the one named last changes fastest.
Arguments:
- start_vecs: float32 [16, 32, 4, 64, 128], P('gx', 'gy'), may hold values from -12 to 12
- force_blocks: bfloat16 [16, 32, 4, 27, 128, 128], P('gx', 'gy'), may hold values from -0.0625 to 0.0625
- slot_offsets: int32 [16, 32, 4, 27], P('gx', 'gy'), may hold values from 0 to 26, each once within a row
Outputs:
- moments: float32 [9, 32], replicated
- last_vecs: float32 [16, 32, 4, 64, 128], P('gx', 'gy')
The draws below stay inside these ranges and needn't reach their ends.
Inputs may be any that keep to these rules, and one draw needn't show every extreme that they name: `slot_offsets`: each tile's 27 slots name the 27 offset codes once each.
All inputs are finite; a program needn't handle non-finite values.
Results may differ from the reference program's by a relative error of at most 0.0085.
Values may be sent and summed in bfloat16 or wider, within the bound.
A program may use at most 64 MiB of HBM per device.

```python
import math
import jax
import jax.numpy as jnp

TILE = 128
VEC = 32
SLOTS = 27
STEPS = 8
TZ = 4
NX = 16
NY = 32


def draw_start_vecs(key, part):
    key = jax.random.fold_in(key, 11)
    shape = (NX, NY, TZ, 2 * VEC, TILE)
    xpos = jnp.arange(NX, dtype=jnp.float32) / float(max(NX - 1, 1))
    ramp = jnp.exp(math.log(3.0) * xpos)[:, None, None, None, None]
    values = jnp.clip(jax.random.normal(key, shape, jnp.float32), -4.0, 4.0) * ramp
    return jnp.clip(values, -12.0, 12.0)


def levels(rng, extent, cuts, low, high):
    gain = 1.0
    for dim, shards_of in cuts:
        draws = jax.random.uniform(jax.random.fold_in(jax.random.fold_in(rng, 6), dim), (shards_of,), jnp.float32, low / len(cuts), high / len(cuts))
        gain = gain * jnp.repeat(jnp.exp(draws), extent[dim] // shards_of).reshape((-1,) + (1,) * (len(extent) - 1 - dim))
    return gain


def gaussian(stream_key, shape, spread, limit, shards=(), held_as=jnp.bfloat16):
    entries = spread * jax.random.normal(stream_key, shape, jnp.float32)
    if shards:
        entries = entries * levels(stream_key, shape, shards, -0.22, 0.18)
    return jnp.clip(entries, -limit, limit).astype(held_as)


def setup_inputs(seed: int = 0) -> dict:
    key_of = jax.random.split(jax.random.key(seed), 4)
    return {
        "start_vecs": draw_start_vecs(jax.random.fold_in(key_of[3], 71), 0),
        "force_blocks": gaussian(key_of[1], (NX, NY, TZ, SLOTS, TILE, TILE), ((9 * SLOTS * TILE) // 4) ** -0.5, 0.0625, ((0, 16), (1, 32))),
        "slot_offsets": jax.vmap(lambda own: jax.random.permutation(own, 27))(jax.random.split(key_of[2], NX * NY * TZ)).reshape((NX, NY, TZ, SLOTS)).astype(jnp.int32),
    }


def offsets_of(code):
    return code // 9 - 1, (code // 3) % 3 - 1, code % 3 - 1


def reorder(force_blocks, slot_offsets):
    codes = jnp.arange(27, dtype=jnp.int32)
    slot_ids = jnp.arange(27, dtype=jnp.int32)
    match = slot_offsets[..., :, None] == codes
    inverse = jnp.sum(jnp.where(match, slot_ids[:, None], 0), axis=-2).astype(jnp.int32)
    return inverse


def apply_operator(vec, force_blocks, inverse):
    rounded = vec.astype(jnp.bfloat16)
    depth = rounded.shape[2]
    padded = jnp.pad(rounded, ((0, 0), (0, 0), (1, 1), (0, 0), (0, 0)))
    total = jnp.zeros(vec.shape, jnp.float32)
    for code in range(27):
        step_x, step_y, step_z = offsets_of(code)
        moved = jnp.roll(padded, (-step_x, -step_y), axis=(0, 1))
        moved = moved[:, :, 1 + step_z:1 + step_z + depth]
        picks = inverse[..., code][..., None, None, None]
        block = jnp.take_along_axis(force_blocks, picks, axis=3)[:, :, :, 0]
        total = total + jnp.einsum("xyzcs,xyzrs->xyzcr", moved.astype(jnp.float32), block.astype(jnp.float32))
    return total


def moment_of(first, current, half, rows_total):
    first_re, first_im = first[:, :, :, :half], first[:, :, :, half:]
    cur_re, cur_im = current[:, :, :, :half], current[:, :, :, half:]
    real_part = jnp.sum(first_re * cur_re + first_im * cur_im, axis=(0, 1, 2, 4))
    return real_part / rows_total


def reference(start_vecs, force_blocks, slot_offsets):
    inverse = reorder(force_blocks, slot_offsets)
    half = start_vecs.shape[3] // 2
    rows_total = float(NX * NY * TZ * TILE)
    previous = start_vecs
    current = apply_operator(start_vecs, force_blocks, inverse)
    moments = [moment_of(start_vecs, start_vecs, half, rows_total), moment_of(start_vecs, current, half, rows_total)]
    for step in range(STEPS - 1):
        following = 2.0 * apply_operator(current, force_blocks, inverse) - previous
        previous, current = current, following
        moments.append(moment_of(start_vecs, current, half, rows_total))
    return jnp.stack(moments), current
```

```python
import jax
import jax.numpy as jnp
from jax import lax
from jax.experimental import pallas as pl
from jax.experimental.pallas import tpu as pltpu
from jax.sharding import PartitionSpec as P

STEPS = 8
TILE = 128
DEPTH = 4
CODES = 27
CHUNKS = 2
HALF = 32
ROWS = HALF // CHUNKS
WIDE = DEPTH * TILE
NX, NY = 16, 32
MESH = pl.DeviceIdType.MESH

MESSAGES = (
    (1, 0, 1, 1, 2),
    (-1, 0, 0, 1, 3),
    (1, 1, 1, 1, 4),
    (1, -1, 1, 1, 5),
    (-1, 1, 0, 1, 6),
    (-1, -1, 0, 1, 7),
    (0, 1, 0, 2, 8),
    (0, -1, 0, 2, 10),
)
SLOTS = 12
SOURCES = ((4, 2, 5, 8, 0, 10, 9, 1, 11), (8, 0, 10, 9, 1, 11, 6, 3, 7))
GROUP_A, GROUP_B = 16, 32


def kernel(
    inverse, start_hbm, blocks_hbm, moments_ref, last_ref,
    start, blocks, mats, buf, vecs, first, staged, landed, sums, turned, pay, gather_a, gather_b,
    load_sem, send, recv, pair_send, pair_recv, a_send, a_recv, b_send, b_recv,
):
    gx, gy = lax.axis_index("gx"), lax.axis_index("gy")
    core = lax.rem(gx, 2)
    other = 1 - core
    chip = gx - core
    z_hi, col_x = gx // 8, lax.rem(gx, 8) // 2
    col_y, z_lo = gy // 4, lax.rem(gy, 4)
    in_a = (z_hi * 4 + z_lo) * 2 + core
    in_b = col_y * 4 + col_x

    def neighbour(dx, dy):
        return (lax.rem(gx + 2 * dx + NX, NX), lax.rem(gy + dy + NY, NY))

    def member_a(m):
        z = m // 2
        return ((z // 4) * 8 + col_x * 2 + lax.rem(m, 2), col_y * 4 + lax.rem(z, 4))

    def member_b(m):
        return (z_hi * 8 + lax.rem(m, 4) * 2 + core, (m // 4) * 4 + z_lo)

    load_vecs = pltpu.make_async_copy(start_hbm, start, load_sem.at[0])
    load_blocks = pltpu.make_async_copy(blocks_hbm, blocks, load_sem.at[1])
    load_vecs.start()
    load_blocks.start()

    barrier = pltpu.get_barrier_semaphore()
    for dx, dy, _, _, _ in MESSAGES:
        pl.semaphore_signal(barrier, inc=1, device_id=neighbour(dx, dy), device_id_type=MESH)

    def greet_a(d, c):
        pl.semaphore_signal(
            barrier, inc=1, device_id=member_a(lax.rem(in_a + d, GROUP_A)), device_id_type=MESH
        )
        return c

    def greet_b(d, c):
        pl.semaphore_signal(
            barrier, inc=1, device_id=member_b(lax.rem(in_b + d, GROUP_B)), device_id_type=MESH
        )
        return c

    lax.fori_loop(1, GROUP_A, greet_a, 0)
    lax.fori_loop(1, GROUP_B, greet_b, 0)

    turned[...] = jnp.zeros_like(turned)
    pay[...] = jnp.zeros_like(pay)
    load_vecs.wait()
    for ch in range(CHUNKS):
        for z in range(DEPTH):
            lanes = slice(z * TILE, (z + 1) * TILE)
            mine = pl.ds(pl.multiple_of(core * HALF + ch * ROWS, ROWS), ROWS)
            theirs = pl.ds(pl.multiple_of(other * HALF + ch * ROWS, ROWS), ROWS)
            first[core, ch, :, lanes] = start[z, mine, :]
            staged[ch, :, lanes] = start[z, theirs, :]

    load_blocks.wait()
    blank = jnp.zeros((TILE, TILE), jnp.bfloat16)
    for j in range(9):
        for z in range(DEPTH):
            part, row = z // 2, (z % 2) * TILE
            for window in range(3):
                dz = part + window - z
                if -1 <= dz <= 1:
                    block = blocks[z * CODES + inverse[z, j * 3 + dz + 1]]
                else:
                    block = blank
                mats[core, j, part, row : row + TILE, window * TILE : (window + 1) * TILE] = block

    pl.semaphore_wait(barrier, len(MESSAGES) + GROUP_A - 1 + GROUP_B - 1)

    partner = (chip + other, gy)
    give_vecs = pltpu.make_async_remote_copy(
        src_ref=staged, dst_ref=first.at[core], send_sem=pair_send.at[0], recv_sem=pair_recv.at[0],
        device_id=partner, device_id_type=MESH,
    )
    give_vecs.start()
    give_mats = pltpu.make_async_remote_copy(
        src_ref=mats.at[core], dst_ref=mats.at[core], send_sem=pair_send.at[1], recv_sem=pair_recv.at[1],
        device_id=partner, device_id_type=MESH,
    )

    def copies(p, ch):
        return [
            pltpu.make_async_remote_copy(
                src_ref=buf.at[p, ch, lo : lo + count],
                dst_ref=buf.at[p, ch, slot : slot + count],
                send_sem=send.at[p, ch, i],
                recv_sem=recv.at[p, ch, i],
                device_id=neighbour(dx, dy),
                device_id_type=MESH,
            )
            for i, (dx, dy, lo, count, slot) in enumerate(MESSAGES)
        ]

    def fold(value):
        return sum(value[:, z * TILE : (z + 1) * TILE] for z in range(DEPTH))

    def row_of_sums():
        return jnp.sum(jnp.transpose(turned[...]), axis=0, keepdims=True)

    give_vecs.wait_recv()
    for ch in range(CHUNKS):
        for a in range(2):
            buf[0, ch, a] = first[a, ch].astype(jnp.bfloat16)
        for copy in copies(0, ch):
            copy.start()
    give_mats.start()
    for ch in range(CHUNKS):
        total = jnp.zeros((ROWS, TILE), jnp.float32)
        for a in range(2):
            value = first[a, ch]
            vecs[0, a, ch] = value
            vecs[1, a, ch] = jnp.zeros_like(value)
            total = total + fold(value * value)
        turned[ch * ROWS : (ch + 1) * ROWS, :] = total
    rows_8 = lax.broadcasted_iota(jnp.int32, (8, TILE), 0)
    pay[...] = jnp.where(rows_8 == 0, row_of_sums(), 0.0)
    give_mats.wait_recv()

    def step(n, carry):
        p = lax.rem(n, 2)
        q = 1 - p
        scale = jnp.where(n == 0, 1.0, 2.0).astype(jnp.float32)
        for ch in range(CHUNKS):
            for copy in copies(p, ch):
                copy.wait_recv()

            @pl.when(n >= 1)
            def _():
                for copy in copies(q, ch):
                    copy.wait_send()

            total = jnp.zeros((ROWS, TILE), jnp.float32)
            for a in range(2):
                for part in range(2):
                    acc = jnp.zeros((ROWS, 2 * TILE), jnp.float32)
                    for j in range(9):
                        acc = acc + lax.dot_general(
                            buf[p, ch, SOURCES[a][j], :, part * TILE : (part + 3) * TILE],
                            mats[a, j, part],
                            (((1,), (1,)), ((), ())),
                            preferred_element_type=jnp.float32,
                        )
                    lanes = slice(part * 2 * TILE, (part + 1) * 2 * TILE)
                    value = scale * acc - vecs[q, a, ch, :, lanes]
                    vecs[q, a, ch, :, lanes] = value
                    buf[q, ch, a, :, lanes] = value.astype(jnp.bfloat16)
                    product = value * first[a, ch, :, lanes]
                    total = total + product[:, :TILE] + product[:, TILE:]

            @pl.when(n < STEPS - 1)
            def _():
                for copy in copies(q, ch):
                    copy.start()

            turned[ch * ROWS : (ch + 1) * ROWS, :] = total

        @pl.when(n < STEPS - 1)
        def _():
            pay[...] = jnp.where(rows_8 == n + 1, row_of_sums(), pay[...])

        return carry

    lax.fori_loop(0, STEPS, step, 0)

    final = STEPS % 2
    give_last = pltpu.make_async_remote_copy(
        src_ref=vecs.at[final, other], dst_ref=landed, send_sem=pair_send.at[2], recv_sem=pair_recv.at[2],
        device_id=partner, device_id_type=MESH,
    )
    give_last.start()

    eighth = pltpu.roll(jnp.broadcast_to(row_of_sums(), (8, TILE)), HALF, 1)
    lanes_8 = lax.broadcasted_iota(jnp.int32, (8, TILE), 1)
    put = (rows_8 == 0) & (lanes_8 >= HALF) & (lanes_8 < 2 * HALF)
    sums[0] = jnp.where(put, eighth, pay[...])

    def share(source, gathered, me, member, size, sent, received):
        def to(d):
            return pltpu.make_async_remote_copy(
                src_ref=source, dst_ref=gathered.at[me], send_sem=sent.at[d], recv_sem=received.at[me],
                device_id=member(lax.rem(me + d, size)), device_id_type=MESH,
            )

        def begin(d, c):
            to(d).start()
            return c

        def finish(d, c):
            who = lax.rem(me + d, size)
            pltpu.make_async_remote_copy(
                src_ref=source, dst_ref=gathered.at[who], send_sem=sent.at[d], recv_sem=received.at[who],
                device_id=member(who), device_id_type=MESH,
            ).wait_recv()
            return c

        def done(d, c):
            to(d).wait_send()
            return c

        lax.fori_loop(1, size, begin, 0)
        gathered[me] = source[...]
        lax.fori_loop(1, size, finish, 0)
        result = jnp.sum(gathered[...], axis=0)
        return result, lambda: lax.fori_loop(1, size, done, 0)

    result_a, done_a = share(sums.at[0], gather_a, in_a, member_a, GROUP_A, a_send, a_recv)
    sums[1] = result_a
    result_b, done_b = share(sums.at[1], gather_b, in_b, member_b, GROUP_B, b_send, b_recv)
    scaled = result_b * (1.0 / (NX * NY * DEPTH * TILE))
    moments_ref[0:8, :] = scaled[:, :HALF]
    moments_ref[8:9, :] = pltpu.roll(scaled, TILE - HALF, 1)[0:1, :HALF]

    give_last.wait_recv()
    for ch in range(CHUNKS):
        for z in range(DEPTH):
            lanes = slice(z * TILE, (z + 1) * TILE)
            mine = pl.ds(pl.multiple_of(core * HALF + ch * ROWS, ROWS), ROWS)
            theirs = pl.ds(pl.multiple_of(other * HALF + ch * ROWS, ROWS), ROWS)
            last_ref[z, mine, :] = vecs[final, core, ch, :, lanes]
            last_ref[z, theirs, :] = landed[ch, :, lanes]

    done_a()
    done_b()
    for copy in (give_vecs, give_mats, give_last):
        copy.wait_send()
    for ch in range(CHUNKS):
        for copy in copies((STEPS - 1) % 2, ch):
            copy.wait_send()


def body(start_vecs, force_blocks, slot_offsets):
    codes = lax.broadcasted_iota(jnp.int32, (DEPTH, CODES, CODES), 2)
    slots = lax.broadcasted_iota(jnp.int32, (DEPTH, CODES, CODES), 1)
    match = slot_offsets.reshape(DEPTH, CODES)[:, :, None] == codes
    inverse = jnp.sum(jnp.where(match, slots, 0), axis=1).astype(jnp.int32)
    vec_shape = (2, CHUNKS, ROWS, WIDE)
    count = len(MESSAGES)
    moments, last = pl.pallas_call(
        kernel,
        out_shape=(
            jax.ShapeDtypeStruct((STEPS + 1, HALF), jnp.float32),
            jax.ShapeDtypeStruct((DEPTH, 2 * HALF, TILE), jnp.float32),
        ),
        in_specs=[
            pl.BlockSpec(memory_space=pltpu.SMEM),
            pl.BlockSpec(memory_space=pl.ANY),
            pl.BlockSpec(memory_space=pl.ANY),
        ],
        out_specs=(pl.BlockSpec(memory_space=pltpu.VMEM), pl.BlockSpec(memory_space=pltpu.VMEM)),
        scratch_shapes=[
            pltpu.VMEM((DEPTH, 2 * HALF, TILE), jnp.float32),
            pltpu.VMEM((DEPTH * CODES, TILE, TILE), jnp.bfloat16),
            pltpu.VMEM((2, 9, 2, 2 * TILE, 3 * TILE), jnp.bfloat16),
            pltpu.VMEM((2, CHUNKS, SLOTS, ROWS, WIDE), jnp.bfloat16),
            pltpu.VMEM((2,) + vec_shape, jnp.float32),
            pltpu.VMEM(vec_shape, jnp.float32),
            pltpu.VMEM(vec_shape[1:], jnp.float32),
            pltpu.VMEM(vec_shape[1:], jnp.float32),
            pltpu.VMEM((2, 8, TILE), jnp.float32),
            pltpu.VMEM((TILE, TILE), jnp.float32),
            pltpu.VMEM((8, TILE), jnp.float32),
            pltpu.VMEM((GROUP_A, 8, TILE), jnp.float32),
            pltpu.VMEM((GROUP_B, 8, TILE), jnp.float32),
            pltpu.SemaphoreType.DMA((2,)),
            pltpu.SemaphoreType.DMA((2, CHUNKS, count)),
            pltpu.SemaphoreType.DMA((2, CHUNKS, count)),
            pltpu.SemaphoreType.DMA((3,)),
            pltpu.SemaphoreType.DMA((3,)),
            pltpu.SemaphoreType.DMA((GROUP_A,)),
            pltpu.SemaphoreType.DMA((GROUP_A,)),
            pltpu.SemaphoreType.DMA((GROUP_B,)),
            pltpu.SemaphoreType.DMA((GROUP_B,)),
        ],
        compiler_params=pltpu.CompilerParams(
            collective_id=0, has_side_effects=True, vmem_limit_bytes=32 << 20
        ),
    )(
        inverse,
        start_vecs.reshape(DEPTH, 2 * HALF, TILE),
        force_blocks.reshape(DEPTH * CODES, TILE, TILE),
    )
    return moments, last.reshape(1, 1, DEPTH, 2 * HALF, TILE)


def solution(mesh):
    in_specs = (
        P("gx", "gy", None, None, None),
        P("gx", "gy", None, None, None, None),
        P("gx", "gy", None, None),
    )
    out_specs = (P(), P("gx", "gy", None, None, None))
    return jax.shard_map(body, mesh=mesh, in_specs=in_specs, out_specs=out_specs, check_vma=False)
```

```python
import jax
import jax.numpy as jnp
from jax import lax
from jax.experimental import pallas as pl
from jax.experimental.pallas import tpu as pltpu
from jax.sharding import PartitionSpec as P

STEPS = 8
TILE = 128
DEPTH = 4
CODES = 27
CHUNKS = 2
HALF = 32
ROWS = HALF // CHUNKS
WIDE = DEPTH * TILE
NX, NY = 16, 32
MESH = pl.DeviceIdType.MESH

MESSAGES = (
    (1, 0, 1, 1, 2),
    (-1, 0, 0, 1, 3),
    (1, 1, 1, 1, 4),
    (1, -1, 1, 1, 5),
    (-1, 1, 0, 1, 6),
    (-1, -1, 0, 1, 7),
    (0, 1, 0, 2, 8),
    (0, -1, 0, 2, 10),
)
SLOTS = 12
SOURCES = ((0, 1, 8, 9, 10, 11, 2, 4, 5), (0, 1, 8, 9, 10, 11, 3, 6, 7))
PLACES = ((4, 7, 3, 6, 5, 8, 1, 0, 2), (1, 4, 0, 3, 2, 5, 7, 6, 8))
GROUPS = (((), 0, 2), ((6, 7), 2, 6), ((0, 1, 2, 3, 4, 5), 6, 9))
GROUP_A, GROUP_B = 16, 32


def window(z):
    return max(z - 1, 0), min(z + 2, DEPTH)


def kernel(
    offsets, start_hbm, blocks_hbm, moments_ref, last_ref,
    start, blocks, mats, buf, vecs, first, staged, landed, sums, turned, pay, gather_a, gather_b,
    load_sem, send, recv, pair_send, pair_recv, a_send, a_recv, b_send, b_recv,
):
    gx, gy = lax.axis_index("gx"), lax.axis_index("gy")
    core = lax.rem(gx, 2)
    other = 1 - core
    chip = gx - core
    z_hi, col_x = gx // 8, lax.rem(gx, 8) // 2
    col_y, z_lo = gy // 4, lax.rem(gy, 4)
    in_a = (z_hi * 4 + z_lo) * 2 + core
    in_b = col_y * 4 + col_x

    def neighbour(dx, dy):
        return (lax.rem(gx + 2 * dx + NX, NX), lax.rem(gy + dy + NY, NY))

    def member_a(m):
        z = m // 2
        return ((z // 4) * 8 + col_x * 2 + lax.rem(m, 2), col_y * 4 + lax.rem(z, 4))

    def member_b(m):
        return (z_hi * 8 + lax.rem(m, 4) * 2 + core, (m // 4) * 4 + z_lo)

    load_vecs = pltpu.make_async_copy(start_hbm, start, load_sem.at[0])
    load_blocks = pltpu.make_async_copy(blocks_hbm, blocks, load_sem.at[1])
    load_vecs.start()
    load_blocks.start()

    barrier = pltpu.get_barrier_semaphore()
    for dx, dy, _, _, _ in MESSAGES:
        pl.semaphore_signal(barrier, inc=1, device_id=neighbour(dx, dy), device_id_type=MESH)

    def greet_a(d, c):
        pl.semaphore_signal(
            barrier, inc=1, device_id=member_a(lax.rem(in_a + d, GROUP_A)), device_id_type=MESH
        )
        return c

    def greet_b(d, c):
        pl.semaphore_signal(
            barrier, inc=1, device_id=member_b(lax.rem(in_b + d, GROUP_B)), device_id_type=MESH
        )
        return c

    lax.fori_loop(1, GROUP_A, greet_a, 0)
    lax.fori_loop(1, GROUP_B, greet_b, 0)

    turned[...] = jnp.zeros_like(turned)
    pay[...] = jnp.zeros_like(pay)
    load_vecs.wait()
    for ch in range(CHUNKS):
        for z in range(DEPTH):
            lanes = slice(z * TILE, (z + 1) * TILE)
            mine = pl.ds(pl.multiple_of(core * HALF + ch * ROWS, ROWS), ROWS)
            theirs = pl.ds(pl.multiple_of(other * HALF + ch * ROWS, ROWS), ROWS)
            first[core, ch, :, lanes] = start[z, mine, :]
            staged[ch, :, lanes] = start[z, theirs, :]

    slots = lax.broadcasted_iota(jnp.int32, (DEPTH, CODES), 1)
    row_z = lax.broadcasted_iota(jnp.int32, (DEPTH, CODES), 0)
    codes = offsets[...]
    eye = jnp.where(
        lax.broadcasted_iota(jnp.int32, (TILE, TILE), 0) == lax.broadcasted_iota(jnp.int32, (TILE, TILE), 1), 1.0, 0.0
    ).astype(jnp.bfloat16)
    load_blocks.wait()
    for z in range(DEPTH):
        low, high = window(z)
        for i in range(9):
            place = jnp.where(core == 0, PLACES[0][i], PLACES[1][i])
            for w in range(high - low):
                code = place * 3 + low + w - z + 1
                pick = jnp.max(jnp.where((codes == code) & (row_z == z), slots, 0))
                block = lax.dot_general(
                    eye, blocks[z * CODES + pick], (((1,), (1,)), ((), ())), preferred_element_type=jnp.float32
                )
                at = (i * (high - low) + w) * TILE
                mats[core, z, at : at + TILE, :] = block.astype(jnp.bfloat16)

    pl.semaphore_wait(barrier, len(MESSAGES) + GROUP_A - 1 + GROUP_B - 1)

    partner = (chip + other, gy)
    give_vecs = pltpu.make_async_remote_copy(
        src_ref=staged, dst_ref=first.at[core], send_sem=pair_send.at[0], recv_sem=pair_recv.at[0],
        device_id=partner, device_id_type=MESH,
    )
    give_vecs.start()
    give_mats = pltpu.make_async_remote_copy(
        src_ref=mats.at[core], dst_ref=mats.at[core], send_sem=pair_send.at[1], recv_sem=pair_recv.at[1],
        device_id=partner, device_id_type=MESH,
    )

    def copies(p, ch):
        return [
            pltpu.make_async_remote_copy(
                src_ref=buf.at[p, ch, lo : lo + count],
                dst_ref=buf.at[p, ch, slot : slot + count],
                send_sem=send.at[p, ch, i],
                recv_sem=recv.at[p, ch, i],
                device_id=neighbour(dx, dy),
                device_id_type=MESH,
            )
            for i, (dx, dy, lo, count, slot) in enumerate(MESSAGES)
        ]

    def fold(value):
        return sum(value[:, z * TILE : (z + 1) * TILE] for z in range(DEPTH))

    def row_of_sums():
        return jnp.sum(jnp.transpose(turned[...]), axis=0, keepdims=True)

    give_vecs.wait_recv()
    for ch in range(CHUNKS):
        for a in range(2):
            buf[0, ch, a] = first[a, ch].astype(jnp.bfloat16)
        for copy in copies(0, ch):
            copy.start()
    give_mats.start()
    for ch in range(CHUNKS):
        total = jnp.zeros((ROWS, TILE), jnp.float32)
        for a in range(2):
            value = first[a, ch]
            vecs[0, a, ch] = value
            vecs[1, a, ch] = jnp.zeros_like(value)
            total = total + fold(value * value)
        turned[ch * ROWS : (ch + 1) * ROWS, :] = total
    rows_8 = lax.broadcasted_iota(jnp.int32, (8, TILE), 0)
    pay[...] = jnp.where(rows_8 == 0, row_of_sums(), 0.0)
    give_mats.wait_recv()

    def step(n, carry):
        p = lax.rem(n, 2)
        q = 1 - p
        scale = jnp.where(n == 0, 1.0, 2.0).astype(jnp.float32)
        for ch in range(CHUNKS):
            accs = [[jnp.zeros((ROWS, TILE), jnp.float32) for _ in range(DEPTH)] for _ in range(2)]
            arriving = copies(p, ch)
            for waits, begin, end in GROUPS:
                for i in waits:
                    arriving[i].wait_recv()
                for a in range(2):
                    pieces = [buf[p, ch, SOURCES[a][i]] for i in range(begin, end)]
                    for z in range(DEPTH):
                        low, high = window(z)
                        wide = (high - low) * TILE
                        left = jnp.concatenate([piece[:, low * TILE : high * TILE] for piece in pieces], axis=1)
                        accs[a][z] = accs[a][z] + jnp.dot(
                            left, mats[a, z, begin * wide : end * wide, :], preferred_element_type=jnp.float32
                        )

            @pl.when(n >= 1)
            def _():
                for copy in copies(q, ch):
                    copy.wait_send()

            total = jnp.zeros((ROWS, TILE), jnp.float32)
            for a in range(2):
                for z in range(DEPTH):
                    lanes = slice(z * TILE, (z + 1) * TILE)
                    value = scale * accs[a][z] - vecs[q, a, ch, :, lanes]
                    vecs[q, a, ch, :, lanes] = value
                    buf[q, ch, a, :, lanes] = value.astype(jnp.bfloat16)
                    total = total + value * first[a, ch, :, lanes]

            @pl.when(n < STEPS - 1)
            def _():
                for copy in copies(q, ch):
                    copy.start()

            turned[ch * ROWS : (ch + 1) * ROWS, :] = total

        @pl.when(n < STEPS - 1)
        def _():
            pay[...] = jnp.where(rows_8 == n + 1, row_of_sums(), pay[...])

        return carry

    lax.fori_loop(0, STEPS, step, 0)

    final = STEPS % 2
    give_last = pltpu.make_async_remote_copy(
        src_ref=vecs.at[final, other], dst_ref=landed, send_sem=pair_send.at[2], recv_sem=pair_recv.at[2],
        device_id=partner, device_id_type=MESH,
    )
    give_last.start()

    eighth = pltpu.roll(jnp.broadcast_to(row_of_sums(), (8, TILE)), HALF, 1)
    lanes_8 = lax.broadcasted_iota(jnp.int32, (8, TILE), 1)
    put = (rows_8 == 0) & (lanes_8 >= HALF) & (lanes_8 < 2 * HALF)
    sums[0] = jnp.where(put, eighth, pay[...])

    def share(source, gathered, me, member, size, sent, received):
        def to(d):
            return pltpu.make_async_remote_copy(
                src_ref=source, dst_ref=gathered.at[me], send_sem=sent.at[d], recv_sem=received.at[me],
                device_id=member(lax.rem(me + d, size)), device_id_type=MESH,
            )

        def begin(d, c):
            to(d).start()
            return c

        def finish(d, c):
            who = lax.rem(me + d, size)
            pltpu.make_async_remote_copy(
                src_ref=source, dst_ref=gathered.at[who], send_sem=sent.at[d], recv_sem=received.at[who],
                device_id=member(who), device_id_type=MESH,
            ).wait_recv()
            return c

        def done(d, c):
            to(d).wait_send()
            return c

        lax.fori_loop(1, size, begin, 0)
        gathered[me] = source[...]
        lax.fori_loop(1, size, finish, 0)
        result = jnp.sum(gathered[...], axis=0)
        return result, lambda: lax.fori_loop(1, size, done, 0)

    result_a, done_a = share(sums.at[0], gather_a, in_a, member_a, GROUP_A, a_send, a_recv)
    sums[1] = result_a
    result_b, done_b = share(sums.at[1], gather_b, in_b, member_b, GROUP_B, b_send, b_recv)
    scaled = result_b * (1.0 / (NX * NY * DEPTH * TILE))
    moments_ref[0:8, :] = scaled[:, :HALF]
    moments_ref[8:9, :] = pltpu.roll(scaled, TILE - HALF, 1)[0:1, :HALF]

    give_last.wait_recv()
    for ch in range(CHUNKS):
        for z in range(DEPTH):
            lanes = slice(z * TILE, (z + 1) * TILE)
            mine = pl.ds(pl.multiple_of(core * HALF + ch * ROWS, ROWS), ROWS)
            theirs = pl.ds(pl.multiple_of(other * HALF + ch * ROWS, ROWS), ROWS)
            last_ref[z, mine, :] = vecs[final, core, ch, :, lanes]
            last_ref[z, theirs, :] = landed[ch, :, lanes]

    done_a()
    done_b()
    for copy in (give_vecs, give_mats, give_last):
        copy.wait_send()
    for ch in range(CHUNKS):
        for copy in copies((STEPS - 1) % 2, ch):
            copy.wait_send()


def body(start_vecs, force_blocks, slot_offsets):
    vec_shape = (2, CHUNKS, ROWS, WIDE)
    count = len(MESSAGES)
    moments, last = pl.pallas_call(
        kernel,
        out_shape=(
            jax.ShapeDtypeStruct((STEPS + 1, HALF), jnp.float32),
            jax.ShapeDtypeStruct((DEPTH, 2 * HALF, TILE), jnp.float32),
        ),
        in_specs=[
            pl.BlockSpec(memory_space=pltpu.VMEM),
            pl.BlockSpec(memory_space=pl.ANY),
            pl.BlockSpec(memory_space=pl.ANY),
        ],
        out_specs=(pl.BlockSpec(memory_space=pltpu.VMEM), pl.BlockSpec(memory_space=pltpu.VMEM)),
        scratch_shapes=[
            pltpu.VMEM((DEPTH, 2 * HALF, TILE), jnp.float32),
            pltpu.VMEM((DEPTH * CODES, TILE, TILE), jnp.bfloat16),
            pltpu.VMEM((2, DEPTH, 27 * TILE, TILE), jnp.bfloat16),
            pltpu.VMEM((2, CHUNKS, SLOTS, ROWS, WIDE), jnp.bfloat16),
            pltpu.VMEM((2,) + vec_shape, jnp.float32),
            pltpu.VMEM(vec_shape, jnp.float32),
            pltpu.VMEM(vec_shape[1:], jnp.float32),
            pltpu.VMEM(vec_shape[1:], jnp.float32),
            pltpu.VMEM((2, 8, TILE), jnp.float32),
            pltpu.VMEM((TILE, TILE), jnp.float32),
            pltpu.VMEM((8, TILE), jnp.float32),
            pltpu.VMEM((GROUP_A, 8, TILE), jnp.float32),
            pltpu.VMEM((GROUP_B, 8, TILE), jnp.float32),
            pltpu.SemaphoreType.DMA((2,)),
            pltpu.SemaphoreType.DMA((2, CHUNKS, count)),
            pltpu.SemaphoreType.DMA((2, CHUNKS, count)),
            pltpu.SemaphoreType.DMA((3,)),
            pltpu.SemaphoreType.DMA((3,)),
            pltpu.SemaphoreType.DMA((GROUP_A,)),
            pltpu.SemaphoreType.DMA((GROUP_A,)),
            pltpu.SemaphoreType.DMA((GROUP_B,)),
            pltpu.SemaphoreType.DMA((GROUP_B,)),
        ],
        compiler_params=pltpu.CompilerParams(
            collective_id=0, has_side_effects=True, vmem_limit_bytes=58 << 20
        ),
    )(
        slot_offsets.reshape(DEPTH, CODES),
        start_vecs.reshape(DEPTH, 2 * HALF, TILE),
        force_blocks.reshape(DEPTH * CODES, TILE, TILE),
    )
    return moments, last.reshape(1, 1, DEPTH, 2 * HALF, TILE)


def solution(mesh):
    in_specs = (
        P("gx", "gy", None, None, None),
        P("gx", "gy", None, None, None, None),
        P("gx", "gy", None, None),
    )
    out_specs = (P(), P("gx", "gy", None, None, None))
    return jax.shard_map(body, mesh=mesh, in_specs=in_specs, out_specs=out_specs, check_vma=False)
```

```python
import jax
import jax.numpy as jnp
from jax import lax
from jax.experimental import pallas as pl
from jax.experimental.pallas import tpu as pltpu
from jax.sharding import PartitionSpec as P

STEPS = 8
TILE = 128
DEPTH = 4
CODES = 27
CHUNKS = 2
HALF = 32
ROWS = HALF // CHUNKS
WIDE = DEPTH * TILE
NX, NY = 16, 32
MESH = pl.DeviceIdType.MESH

MESSAGES = (
    (1, 0, 1, 1, 2),
    (-1, 0, 0, 1, 3),
    (1, 1, 1, 1, 4),
    (1, -1, 1, 1, 5),
    (-1, 1, 0, 1, 6),
    (-1, -1, 0, 1, 7),
    (0, 1, 0, 2, 8),
    (0, -1, 0, 2, 10),
)
SLOTS = 12
SOURCES = ((0, 1, 8, 9, 10, 11, 2, 4, 5), (0, 1, 8, 9, 10, 11, 3, 6, 7))
PLACES = ((4, 7, 3, 6, 5, 8, 1, 0, 2), (1, 4, 0, 3, 2, 5, 7, 6, 8))
GROUPS = (((), 0, 2), ((6, 7), 2, 6), ((0, 1, 2, 3, 4, 5), 6, 9))
GROUP_A, GROUP_B = 16, 32


def hops(step, size):
    return min(step, size - step)


STEPS_A = sorted(
    ((z, c) for z in range(8) for c in range(2) if z or c), key=lambda s: -2 * hops(s[0], 8) - s[1]
)
STEPS_B = sorted(
    ((y, x) for y in range(8) for x in range(4) if y or x), key=lambda s: -hops(s[0], 8) - hops(s[1], 4)
)


def window(z):
    return max(z - 1, 0), min(z + 2, DEPTH)


def kernel(
    offsets, start_hbm, blocks_hbm, moments_ref, last_ref,
    start, blocks, mats, buf, vecs, first, own, staged, landed, sums, turned, gather_a, gather_b,
    load_sem, send, recv, pair_send, pair_recv, a_send, a_recv, b_send, b_recv,
):
    gx, gy = lax.axis_index("gx"), lax.axis_index("gy")
    core = lax.rem(gx, 2)
    other = 1 - core
    chip = gx // 2
    half = lax.rem(core + chip + gy, 2)
    z_hi, col_x = gx // 8, lax.rem(gx, 8) // 2
    col_y, z_lo = gy // 4, lax.rem(gy, 4)
    in_a = (z_hi * 4 + z_lo) * 2 + core
    in_b = col_y * 4 + col_x

    def chip_at(dx, dy):
        return lax.rem(chip + dx + NX // 2, NX // 2), lax.rem(gy + dy + NY, NY)

    def neighbour(dx, dy):
        x, y = chip_at(dx, dy)
        return (2 * x + (core if (dx + dy) % 2 == 0 else other), y)

    def member_a(step):
        z, c = lax.rem(z_hi * 4 + z_lo + step[0], 8), lax.rem(core + step[1], 2)
        return z * 2 + c, ((z // 4) * 8 + col_x * 2 + c, col_y * 4 + lax.rem(z, 4))

    def member_b(step):
        y, x = lax.rem(col_y + step[0], 8), lax.rem(col_x + step[1], 4)
        return y * 4 + x, (z_hi * 8 + x * 2 + core, y * 4 + z_lo)

    load_vecs = pltpu.make_async_copy(start_hbm, start, load_sem.at[0])
    load_blocks = pltpu.make_async_copy(blocks_hbm, blocks, load_sem.at[1])
    load_vecs.start()
    load_blocks.start()

    barrier = pltpu.get_barrier_semaphore()

    def greet(device):
        pl.semaphore_signal(barrier, inc=1, device_id=device, device_id_type=MESH)

    for dx, dy, _, _, _ in MESSAGES:
        x, y = chip_at(dx, dy)
        for c in range(2):
            greet((2 * x + c, y))
    for step in STEPS_B:
        greet(member_b(step)[1])
    for step in STEPS_A:
        greet(member_a(step)[1])

    turned[...] = jnp.zeros_like(turned)
    load_vecs.wait()
    for ch in range(CHUNKS):
        for z in range(DEPTH):
            lanes = slice(z * TILE, (z + 1) * TILE)
            mine = pl.ds(pl.multiple_of(half * HALF + ch * ROWS, ROWS), ROWS)
            theirs = pl.ds(pl.multiple_of((1 - half) * HALF + ch * ROWS, ROWS), ROWS)
            first[core, ch, :, lanes] = start[z, mine, :]
            staged[ch, :, lanes] = start[z, theirs, :]
            for h in range(2):
                low = h * HALF + ch * ROWS
                own[h, ch, 0, :, lanes] = start[z, low : low + ROWS, :].astype(jnp.bfloat16)

    slots = lax.broadcasted_iota(jnp.int32, (DEPTH, CODES), 1)
    row_z = lax.broadcasted_iota(jnp.int32, (DEPTH, CODES), 0)
    codes = offsets[...]
    eye = jnp.where(
        lax.broadcasted_iota(jnp.int32, (TILE, TILE), 0) == lax.broadcasted_iota(jnp.int32, (TILE, TILE), 1), 1.0, 0.0
    ).astype(jnp.bfloat16)
    load_blocks.wait()
    for z in range(DEPTH):
        low, high = window(z)
        for i in range(9):
            place = jnp.where(core == 0, PLACES[0][i], PLACES[1][i])
            for w in range(high - low):
                code = place * 3 + low + w - z + 1
                pick = jnp.max(jnp.where((codes == code) & (row_z == z), slots, 0))
                block = lax.dot_general(
                    eye, blocks[z * CODES + pick], (((1,), (1,)), ((), ())), preferred_element_type=jnp.float32
                )
                at = (i * (high - low) + w) * TILE
                mats[core, z, at : at + TILE, :] = block.astype(jnp.bfloat16)

    pl.semaphore_wait(barrier, 2 * len(MESSAGES) + GROUP_A - 1 + GROUP_B - 1)

    side = 2 * core - 1
    first_sends = []
    for dx, dy, slot, receives, sends in (
        (side, 0, 3 - core, 1 - core, (0, 1)),
        (side, 1, 6 - 2 * core, 4 - 2 * core, (2, 3)),
        (side, -1, 7 - 2 * core, 5 - 2 * core, (4, 5)),
        (0, 1, 8 + core, 6, (6, 6)),
        (0, -1, 10 + core, 7, (7, 7)),
    ):
        x, y = chip_at(dx, dy)
        for c in range(2):
            first_sends.append((2 * x + c, y, lax.rem(c + x + y, 2), slot, receives, sends[c]))
    for ch in range(CHUNKS):
        for x, y, h, slot, receives, sends in first_sends:
            pltpu.make_async_remote_copy(
                src_ref=own.at[h, ch],
                dst_ref=buf.at[0, ch, pl.ds(slot, 1)],
                send_sem=send.at[0, ch, sends],
                recv_sem=recv.at[0, ch, receives],
                device_id=(x, y),
                device_id_type=MESH,
            ).start()

    partner = (2 * chip + other, gy)
    give_vecs = pltpu.make_async_remote_copy(
        src_ref=staged, dst_ref=first.at[core], send_sem=pair_send.at[0], recv_sem=pair_recv.at[0],
        device_id=partner, device_id_type=MESH,
    )
    give_vecs.start()
    give_mats = pltpu.make_async_remote_copy(
        src_ref=mats.at[core], dst_ref=mats.at[core], send_sem=pair_send.at[1], recv_sem=pair_recv.at[1],
        device_id=partner, device_id_type=MESH,
    )

    def copies(p, ch):
        return [
            pltpu.make_async_remote_copy(
                src_ref=buf.at[p, ch, lo : lo + count],
                dst_ref=buf.at[p, ch, slot : slot + count],
                send_sem=send.at[p, ch, i],
                recv_sem=recv.at[p, ch, i],
                device_id=neighbour(dx, dy),
                device_id_type=MESH,
            )
            for i, (dx, dy, lo, count, slot) in enumerate(MESSAGES)
        ]

    def fold(value):
        return sum(value[:, z * TILE : (z + 1) * TILE] for z in range(DEPTH))

    def row_of_sums(i):
        return jnp.sum(jnp.transpose(turned[i]), axis=0, keepdims=True)

    give_mats.start()
    give_vecs.wait_recv()
    for ch in range(CHUNKS):
        total = jnp.zeros((ROWS, TILE), jnp.float32)
        for a in range(2):
            value = first[a, ch]
            buf[0, ch, a] = value.astype(jnp.bfloat16)
            vecs[0, a, ch] = value
            vecs[1, a, ch] = jnp.zeros_like(value)
            total = total + fold(value * value)
        turned[0, ch * ROWS : (ch + 1) * ROWS, :] = total
    give_mats.wait_recv()

    def step(n, carry):
        p = lax.rem(n, 2)
        q = 1 - p
        scale = jnp.where(n == 0, 1.0, 2.0).astype(jnp.float32)

        for ch in range(CHUNKS):
            accs = [[jnp.zeros((ROWS, TILE), jnp.float32) for _ in range(DEPTH)] for _ in range(2)]
            arriving = copies(p, ch)
            for waits, begin, end in GROUPS:
                for i in waits:
                    arriving[i].wait_recv()
                for a in range(2):
                    pieces = [buf[p, ch, SOURCES[a][i]] for i in range(begin, end)]
                    for z in range(DEPTH):
                        low, high = window(z)
                        wide = (high - low) * TILE
                        left = jnp.concatenate([piece[:, low * TILE : high * TILE] for piece in pieces], axis=1)
                        accs[a][z] = accs[a][z] + jnp.dot(
                            left, mats[a, z, begin * wide : end * wide, :], preferred_element_type=jnp.float32
                        )

            @pl.when(n >= 1)
            def _():
                for copy in copies(q, ch):
                    copy.wait_send()

            for a in range(2):
                for z in range(DEPTH):
                    lanes = slice(z * TILE, (z + 1) * TILE)
                    value = scale * accs[a][z] - vecs[q, a, ch, :, lanes]
                    vecs[q, a, ch, :, lanes] = value
                    buf[q, ch, a, :, lanes] = value.astype(jnp.bfloat16)

            @pl.when(n < STEPS - 1)
            def _():
                for copy in copies(q, ch):
                    copy.start()

            total = sum(fold(vecs[q, a, ch] * first[a, ch]) for a in range(2))
            at = pl.multiple_of(lax.rem(n + 1, 4) * HALF + ch * ROWS, ROWS)
            turned[(n + 1) // 4, pl.ds(at, ROWS), :] = total

        @pl.when(n == STEPS - 2)
        def _():
            for i in range(2):
                sums[0, :, i * TILE : (i + 1) * TILE] = row_of_sums(i)

        return carry

    lax.fori_loop(0, STEPS, step, 0)

    final = STEPS % 2
    give_last = pltpu.make_async_remote_copy(
        src_ref=vecs.at[final, other], dst_ref=landed, send_sem=pair_send.at[2], recv_sem=pair_recv.at[2],
        device_id=partner, device_id_type=MESH,
    )
    give_last.start()

    sums[0, :, 2 * TILE :] = row_of_sums(2)

    def share(source, gathered, me, member, steps, sent, received, meanwhile):
        partners = [member(step) for step in steps]

        def copy(i, slot):
            return pltpu.make_async_remote_copy(
                src_ref=source, dst_ref=gathered.at[slot], send_sem=sent.at[i], recv_sem=received.at[slot],
                device_id=partners[i][1], device_id_type=MESH,
            )

        for i in range(len(steps)):
            copy(i, me).start()
        gathered[me] = source[...]
        meanwhile()
        for i in range(len(steps)):
            copy(i, me).wait_send()
        for i, (who, _) in enumerate(partners):
            copy(i, who).wait_recv()
        return jnp.sum(gathered[...], axis=0)

    def assemble():
        for ch in range(CHUNKS):
            for z in range(DEPTH):
                lanes = slice(z * TILE, (z + 1) * TILE)
                mine = pl.ds(pl.multiple_of(half * HALF + ch * ROWS, ROWS), ROWS)
                last_ref[z, mine, :] = vecs[final, core, ch, :, lanes]
        for copy in (give_vecs, give_mats):
            copy.wait_send()
        for ch in range(CHUNKS):
            for copy in copies((STEPS - 1) % 2, ch):
                copy.wait_send()

    def assemble_rest():
        give_last.wait_recv()
        for ch in range(CHUNKS):
            for z in range(DEPTH):
                lanes = slice(z * TILE, (z + 1) * TILE)
                theirs = pl.ds(pl.multiple_of((1 - half) * HALF + ch * ROWS, ROWS), ROWS)
                last_ref[z, theirs, :] = landed[ch, :, lanes]
        give_last.wait_send()

    sums[1] = share(sums.at[0], gather_a, in_a, member_a, STEPS_A, a_send, a_recv, assemble)
    result_b = share(sums.at[1], gather_b, in_b, member_b, STEPS_B, b_send, b_recv, assemble_rest)
    scaled = result_b * (1.0 / (NX * NY * DEPTH * TILE))
    for n in range(STEPS + 1):
        row = jnp.broadcast_to(scaled[:, n // 4 * TILE : (n // 4 + 1) * TILE], (8, TILE))
        if n % 4:
            row = pltpu.roll(row, TILE - n % 4 * HALF, 1)
        moments_ref[n : n + 1, :] = row[0:1, :HALF]


def body(start_vecs, force_blocks, slot_offsets):
    vec_shape = (2, CHUNKS, ROWS, WIDE)
    count = len(MESSAGES)
    moments, last = pl.pallas_call(
        kernel,
        out_shape=(
            jax.ShapeDtypeStruct((STEPS + 1, HALF), jnp.float32),
            jax.ShapeDtypeStruct((DEPTH, 2 * HALF, TILE), jnp.float32),
        ),
        in_specs=[
            pl.BlockSpec(memory_space=pltpu.VMEM),
            pl.BlockSpec(memory_space=pltpu.HBM),
            pl.BlockSpec(memory_space=pltpu.HBM),
        ],
        out_specs=(pl.BlockSpec(memory_space=pltpu.VMEM), pl.BlockSpec(memory_space=pltpu.VMEM)),
        scratch_shapes=[
            pltpu.VMEM((DEPTH, 2 * HALF, TILE), jnp.float32),
            pltpu.VMEM((DEPTH * CODES, TILE, TILE), jnp.bfloat16),
            pltpu.VMEM((2, DEPTH, 27 * TILE, TILE), jnp.bfloat16),
            pltpu.VMEM((2, CHUNKS, SLOTS, ROWS, WIDE), jnp.bfloat16),
            pltpu.VMEM((2,) + vec_shape, jnp.float32),
            pltpu.VMEM(vec_shape, jnp.float32),
            pltpu.VMEM((2, CHUNKS, 1, ROWS, WIDE), jnp.bfloat16),
            pltpu.VMEM(vec_shape[1:], jnp.float32),
            pltpu.VMEM(vec_shape[1:], jnp.float32),
            pltpu.VMEM((2, 1, 3 * TILE), jnp.float32),
            pltpu.VMEM((3, TILE, TILE), jnp.float32),
            pltpu.VMEM((GROUP_A, 1, 3 * TILE), jnp.float32),
            pltpu.VMEM((GROUP_B, 1, 3 * TILE), jnp.float32),
            pltpu.SemaphoreType.DMA((2,)),
            pltpu.SemaphoreType.DMA((2, CHUNKS, count)),
            pltpu.SemaphoreType.DMA((2, CHUNKS, count)),
            pltpu.SemaphoreType.DMA((3,)),
            pltpu.SemaphoreType.DMA((3,)),
            pltpu.SemaphoreType.DMA((GROUP_A,)),
            pltpu.SemaphoreType.DMA((GROUP_A,)),
            pltpu.SemaphoreType.DMA((GROUP_B,)),
            pltpu.SemaphoreType.DMA((GROUP_B,)),
        ],
        compiler_params=pltpu.CompilerParams(
            collective_id=0, has_side_effects=True, vmem_limit_bytes=52 << 20
        ),
    )(
        slot_offsets.reshape(DEPTH, CODES),
        start_vecs.reshape(DEPTH, 2 * HALF, TILE),
        force_blocks.reshape(DEPTH * CODES, TILE, TILE),
    )
    return moments, last.reshape(1, 1, DEPTH, 2 * HALF, TILE)


def solution(mesh):
    in_specs = (
        P("gx", "gy", None, None, None),
        P("gx", "gy", None, None, None, None),
        P("gx", "gy", None, None),
    )
    out_specs = (P(), P("gx", "gy", None, None, None))
    return jax.shard_map(body, mesh=mesh, in_specs=in_specs, out_specs=out_specs, check_vma=False)
```

```python
import jax
import jax.numpy as jnp
from jax import lax
from jax.experimental import pallas as pl
from jax.experimental.pallas import tpu as pltpu
from jax.sharding import PartitionSpec as P

STEPS = 8
TILE = 128
DEPTH = 4
CODES = 27
CHUNKS = 2
HALF = 32
ROWS = HALF // CHUNKS
WIDE = DEPTH * TILE
NX, NY = 16, 32
MESH = pl.DeviceIdType.MESH

MESSAGES = (
    (1, 0, 1, 1, 2),
    (-1, 0, 0, 1, 3),
    (1, 1, 1, 1, 4),
    (1, -1, 1, 1, 5),
    (-1, 1, 0, 1, 6),
    (-1, -1, 0, 1, 7),
    (0, 1, 0, 2, 8),
    (0, -1, 0, 2, 10),
)
SLOTS = 12
SOURCES = ((0, 1, 8, 9, 10, 11, 2, 4, 5), (0, 1, 8, 9, 10, 11, 3, 6, 7))
PLACES = ((4, 7, 3, 6, 5, 8, 1, 0, 2), (1, 4, 0, 3, 2, 5, 7, 6, 8))
GROUPS = (((), 0, 2), ((6, 7), 2, 6), ((0, 1, 2, 3, 4, 5), 6, 9))
LEAVING = ((1, 4, 5, 6, 7), (0, 2, 3))
GROUP_A, GROUP_B = 16, 32


def hops(step, size):
    return min(step, size - step)


STEPS_A = sorted(
    ((z, c) for z in range(8) for c in range(2) if z or c), key=lambda s: -2 * hops(s[0], 8) - s[1]
)
STEPS_B = sorted(
    ((y, x) for y in range(8) for x in range(4) if y or x), key=lambda s: -hops(s[0], 8) - hops(s[1], 4)
)


def window(z):
    return max(z - 1, 0), min(z + 2, DEPTH)


def kernel(
    offsets, start_hbm, blocks_hbm, moments_ref, last_ref,
    start, blocks, mats, buf, vecs, first, own, staged, landed, sums, turned, gather_a, gather_b,
    load_sem, send, recv, pair_send, pair_recv, a_send, a_recv, b_send, b_recv,
):
    gx, gy = lax.axis_index("gx"), lax.axis_index("gy")
    core = lax.rem(gx, 2)
    other = 1 - core
    chip = gx // 2
    half = lax.rem(core + chip + gy, 2)
    z_hi, col_x = gx // 8, lax.rem(gx, 8) // 2
    col_y, z_lo = gy // 4, lax.rem(gy, 4)
    in_a = (z_hi * 4 + z_lo) * 2 + core
    in_b = col_y * 4 + col_x

    def chip_at(dx, dy):
        return lax.rem(chip + dx + NX // 2, NX // 2), lax.rem(gy + dy + NY, NY)

    def neighbour(dx, dy):
        x, y = chip_at(dx, dy)
        return (2 * x + (core if (dx + dy) % 2 == 0 else other), y)

    def member_a(step):
        z, c = lax.rem(z_hi * 4 + z_lo + step[0], 8), lax.rem(core + step[1], 2)
        return z * 2 + c, ((z // 4) * 8 + col_x * 2 + c, col_y * 4 + lax.rem(z, 4))

    def member_b(step):
        y, x = lax.rem(col_y + step[0], 8), lax.rem(col_x + step[1], 4)
        return y * 4 + x, (z_hi * 8 + x * 2 + core, y * 4 + z_lo)

    load_vecs = pltpu.make_async_copy(start_hbm, start, load_sem.at[0])
    load_blocks = pltpu.make_async_copy(blocks_hbm, blocks, load_sem.at[1])
    load_vecs.start()
    load_blocks.start()

    barrier = pltpu.get_barrier_semaphore()

    def greet(device):
        pl.semaphore_signal(barrier, inc=1, device_id=device, device_id_type=MESH)

    for dx, dy, _, _, _ in MESSAGES:
        x, y = chip_at(dx, dy)
        for c in range(2):
            greet((2 * x + c, y))
    for step in STEPS_B:
        greet(member_b(step)[1])
    for step in STEPS_A:
        greet(member_a(step)[1])

    turned[...] = jnp.zeros_like(turned)
    load_vecs.wait()
    for ch in range(CHUNKS):
        for z in range(DEPTH):
            lanes = slice(z * TILE, (z + 1) * TILE)
            mine = pl.ds(pl.multiple_of(half * HALF + ch * ROWS, ROWS), ROWS)
            theirs = pl.ds(pl.multiple_of((1 - half) * HALF + ch * ROWS, ROWS), ROWS)
            first[core, ch, :, lanes] = start[z, mine, :]
            staged[ch, :, lanes] = start[z, theirs, :]
            for h in range(2):
                low = h * HALF + ch * ROWS
                own[h, ch, 0, :, lanes] = start[z, low : low + ROWS, :].astype(jnp.bfloat16)

    slots = lax.broadcasted_iota(jnp.int32, (DEPTH, CODES), 1)
    row_z = lax.broadcasted_iota(jnp.int32, (DEPTH, CODES), 0)
    codes = offsets[...]
    eye = jnp.where(
        lax.broadcasted_iota(jnp.int32, (TILE, TILE), 0) == lax.broadcasted_iota(jnp.int32, (TILE, TILE), 1), 1.0, 0.0
    ).astype(jnp.bfloat16)
    load_blocks.wait()
    for z in range(DEPTH):
        low, high = window(z)
        for i in range(9):
            place = jnp.where(core == 0, PLACES[0][i], PLACES[1][i])
            for w in range(high - low):
                code = place * 3 + low + w - z + 1
                pick = jnp.max(jnp.where((codes == code) & (row_z == z), slots, 0))
                block = lax.dot_general(
                    eye, blocks[z * CODES + pick], (((1,), (1,)), ((), ())), preferred_element_type=jnp.float32
                )
                at = (i * (high - low) + w) * TILE
                mats[core, z, at : at + TILE, :] = block.astype(jnp.bfloat16)

    pl.semaphore_wait(barrier, 2 * len(MESSAGES) + GROUP_A - 1 + GROUP_B - 1)

    side = 2 * core - 1
    first_sends = []
    for dx, dy, slot, receives, sends in (
        (side, 0, 3 - core, 1 - core, (0, 1)),
        (side, 1, 6 - 2 * core, 4 - 2 * core, (2, 3)),
        (side, -1, 7 - 2 * core, 5 - 2 * core, (4, 5)),
        (0, 1, 8 + core, 6, (6, 6)),
        (0, -1, 10 + core, 7, (7, 7)),
    ):
        x, y = chip_at(dx, dy)
        for c in range(2):
            first_sends.append((2 * x + c, y, lax.rem(c + x + y, 2), slot, receives, sends[c]))
    for ch in range(CHUNKS):
        for x, y, h, slot, receives, sends in first_sends:
            pltpu.make_async_remote_copy(
                src_ref=own.at[h, ch],
                dst_ref=buf.at[0, ch, pl.ds(slot, 1)],
                send_sem=send.at[0, ch, sends],
                recv_sem=recv.at[0, ch, receives],
                device_id=(x, y),
                device_id_type=MESH,
            ).start()

    partner = (2 * chip + other, gy)
    give_vecs = pltpu.make_async_remote_copy(
        src_ref=staged, dst_ref=first.at[core], send_sem=pair_send.at[0], recv_sem=pair_recv.at[0],
        device_id=partner, device_id_type=MESH,
    )
    give_vecs.start()
    give_mats = pltpu.make_async_remote_copy(
        src_ref=mats.at[core], dst_ref=mats.at[core], send_sem=pair_send.at[1], recv_sem=pair_recv.at[1],
        device_id=partner, device_id_type=MESH,
    )

    def copies(p, ch):
        return [
            pltpu.make_async_remote_copy(
                src_ref=buf.at[p, ch, lo : lo + count],
                dst_ref=buf.at[p, ch, slot : slot + count],
                send_sem=send.at[p, ch, i],
                recv_sem=recv.at[p, ch, i],
                device_id=neighbour(dx, dy),
                device_id_type=MESH,
            )
            for i, (dx, dy, lo, count, slot) in enumerate(MESSAGES)
        ]

    def fold(value):
        return sum(value[:, z * TILE : (z + 1) * TILE] for z in range(DEPTH))

    def row_of_sums(i):
        return jnp.sum(jnp.transpose(turned[i]), axis=0, keepdims=True)

    give_mats.start()
    give_vecs.wait_recv()
    for ch in range(CHUNKS):
        total = jnp.zeros((ROWS, TILE), jnp.float32)
        for a in range(2):
            value = first[a, ch]
            buf[0, ch, a] = value.astype(jnp.bfloat16)
            vecs[0, a, ch] = value
            total = total + fold(value * value)
        turned[0, ch * ROWS : (ch + 1) * ROWS, :] = total
    give_mats.wait_recv()

    def products(p, ch, a, group, accs):
        _, begin, end = GROUPS[group]
        pieces = [buf[p, ch, SOURCES[a][i]] for i in range(begin, end)]
        for z in range(DEPTH):
            low, high = window(z)
            wide = (high - low) * TILE
            left = jnp.concatenate([piece[:, low * TILE : high * TILE] for piece in pieces], axis=1)
            part = jnp.dot(left, mats[a, z, begin * wide : end * wide, :], preferred_element_type=jnp.float32)
            accs[z] = part if accs[z] is None else accs[z] + part

    def step(n, p, is_first, is_last):
        q = 1 - p
        for ch in range(CHUNKS):
            accs = [[None] * DEPTH for _ in range(2)]
            arriving = copies(p, ch)
            for group in range(2):
                for i in GROUPS[group][0]:
                    arriving[i].wait_recv()
                for a in range(2):
                    products(p, ch, a, group, accs[a])
            if not is_first:
                for copy in copies(q, ch):
                    copy.wait_send()
            for i in GROUPS[2][0]:
                arriving[i].wait_recv()
            leaving = copies(q, ch)
            for a in (1, 0):
                products(p, ch, a, 2, accs[a])
                for z in range(DEPTH):
                    lanes = slice(z * TILE, (z + 1) * TILE)
                    value = accs[a][z] if is_first else 2.0 * accs[a][z] - vecs[q, a, ch, :, lanes]
                    vecs[q, a, ch, :, lanes] = value
                    if not is_last:
                        buf[q, ch, a, :, lanes] = value.astype(jnp.bfloat16)
                if not is_last:
                    for i in LEAVING[a]:
                        leaving[i].start()
            total = sum(fold(vecs[q, a, ch] * first[a, ch]) for a in range(2))
            at = lax.rem(n + 1, 4) * HALF + ch * ROWS
            turned[(n + 1) // 4, pl.ds(pl.multiple_of(at, ROWS), ROWS), :] = total

    def middle(n, carry):
        step(n, lax.rem(n, 2), False, False)
        return carry

    step(jnp.int32(0), 0, True, False)
    lax.fori_loop(1, STEPS - 1, middle, 0)
    for i in range(2):
        sums[0, :, i * TILE : (i + 1) * TILE] = row_of_sums(i)
    step(jnp.int32(STEPS - 1), (STEPS - 1) % 2, False, True)

    final = STEPS % 2
    give_last = pltpu.make_async_remote_copy(
        src_ref=vecs.at[final, other], dst_ref=landed, send_sem=pair_send.at[2], recv_sem=pair_recv.at[2],
        device_id=partner, device_id_type=MESH,
    )
    give_last.start()

    sums[0, :, 2 * TILE :] = row_of_sums(2)

    def share(source, gathered, me, member, steps, sent, received, meanwhile):
        partners = [member(step) for step in steps]

        def copy(i, slot):
            return pltpu.make_async_remote_copy(
                src_ref=source, dst_ref=gathered.at[slot], send_sem=sent.at[i], recv_sem=received.at[slot],
                device_id=partners[i][1], device_id_type=MESH,
            )

        for i in range(len(steps)):
            copy(i, me).start()
        gathered[me] = source[...]
        meanwhile()
        for i in range(len(steps)):
            copy(i, me).wait_send()
        for i, (who, _) in enumerate(partners):
            copy(i, who).wait_recv()
        return jnp.sum(gathered[...], axis=0)

    def assemble():
        for ch in range(CHUNKS):
            for z in range(DEPTH):
                lanes = slice(z * TILE, (z + 1) * TILE)
                mine = pl.ds(pl.multiple_of(half * HALF + ch * ROWS, ROWS), ROWS)
                last_ref[z, mine, :] = vecs[final, core, ch, :, lanes]
        for copy in (give_vecs, give_mats):
            copy.wait_send()
        for ch in range(CHUNKS):
            for copy in copies((STEPS - 1) % 2, ch):
                copy.wait_send()

    def assemble_rest():
        give_last.wait_recv()
        for ch in range(CHUNKS):
            for z in range(DEPTH):
                lanes = slice(z * TILE, (z + 1) * TILE)
                theirs = pl.ds(pl.multiple_of((1 - half) * HALF + ch * ROWS, ROWS), ROWS)
                last_ref[z, theirs, :] = landed[ch, :, lanes]
        give_last.wait_send()

    sums[1] = share(sums.at[0], gather_a, in_a, member_a, STEPS_A, a_send, a_recv, assemble)
    result_b = share(sums.at[1], gather_b, in_b, member_b, STEPS_B, b_send, b_recv, assemble_rest)
    scaled = result_b * (1.0 / (NX * NY * DEPTH * TILE))
    for n in range(STEPS + 1):
        row = jnp.broadcast_to(scaled[:, n // 4 * TILE : (n // 4 + 1) * TILE], (8, TILE))
        if n % 4:
            row = pltpu.roll(row, TILE - n % 4 * HALF, 1)
        moments_ref[n : n + 1, :] = row[0:1, :HALF]


def body(start_vecs, force_blocks, slot_offsets):
    vec_shape = (2, CHUNKS, ROWS, WIDE)
    count = len(MESSAGES)
    moments, last = pl.pallas_call(
        kernel,
        out_shape=(
            jax.ShapeDtypeStruct((STEPS + 1, HALF), jnp.float32),
            jax.ShapeDtypeStruct((DEPTH, 2 * HALF, TILE), jnp.float32),
        ),
        in_specs=[
            pl.BlockSpec(memory_space=pltpu.VMEM),
            pl.BlockSpec(memory_space=pltpu.HBM),
            pl.BlockSpec(memory_space=pltpu.HBM),
        ],
        out_specs=(pl.BlockSpec(memory_space=pltpu.VMEM), pl.BlockSpec(memory_space=pltpu.VMEM)),
        scratch_shapes=[
            pltpu.VMEM((DEPTH, 2 * HALF, TILE), jnp.float32),
            pltpu.VMEM((DEPTH * CODES, TILE, TILE), jnp.bfloat16),
            pltpu.VMEM((2, DEPTH, 27 * TILE, TILE), jnp.bfloat16),
            pltpu.VMEM((2, CHUNKS, SLOTS, ROWS, WIDE), jnp.bfloat16),
            pltpu.VMEM((2,) + vec_shape, jnp.float32),
            pltpu.VMEM(vec_shape, jnp.float32),
            pltpu.VMEM((2, CHUNKS, 1, ROWS, WIDE), jnp.bfloat16),
            pltpu.VMEM(vec_shape[1:], jnp.float32),
            pltpu.VMEM(vec_shape[1:], jnp.float32),
            pltpu.VMEM((2, 1, 3 * TILE), jnp.float32),
            pltpu.VMEM((3, TILE, TILE), jnp.float32),
            pltpu.VMEM((GROUP_A, 1, 3 * TILE), jnp.float32),
            pltpu.VMEM((GROUP_B, 1, 3 * TILE), jnp.float32),
            pltpu.SemaphoreType.DMA((2,)),
            pltpu.SemaphoreType.DMA((2, CHUNKS, count)),
            pltpu.SemaphoreType.DMA((2, CHUNKS, count)),
            pltpu.SemaphoreType.DMA((3,)),
            pltpu.SemaphoreType.DMA((3,)),
            pltpu.SemaphoreType.DMA((GROUP_A,)),
            pltpu.SemaphoreType.DMA((GROUP_A,)),
            pltpu.SemaphoreType.DMA((GROUP_B,)),
            pltpu.SemaphoreType.DMA((GROUP_B,)),
        ],
        compiler_params=pltpu.CompilerParams(
            collective_id=0, has_side_effects=True, vmem_limit_bytes=55008 << 10
        ),
    )(
        slot_offsets.reshape(DEPTH, CODES),
        start_vecs.reshape(DEPTH, 2 * HALF, TILE),
        force_blocks.reshape(DEPTH * CODES, TILE, TILE),
    )
    return moments, last.reshape(1, 1, DEPTH, 2 * HALF, TILE)


def solution(mesh):
    in_specs = (
        P("gx", "gy", None, None, None),
        P("gx", "gy", None, None, None, None),
        P("gx", "gy", None, None),
    )
    out_specs = (P(), P("gx", "gy", None, None, None))
    return jax.shard_map(body, mesh=mesh, in_specs=in_specs, out_specs=out_specs, check_vma=False)
```

```python
import jax
import jax.numpy as jnp
from jax import lax
from jax.experimental import pallas as pl
from jax.experimental.pallas import tpu as pltpu
from jax.sharding import PartitionSpec as P

STEPS = 8
TILE = 128
DEPTH = 4
CODES = 27
CHUNKS = 2
HALF = 32
ROWS = HALF // CHUNKS
WIDE = DEPTH * TILE
NX, NY = 16, 32
MESH = pl.DeviceIdType.MESH

MESSAGES = (
    (1, 0, 1, 1, 2),
    (-1, 0, 0, 1, 3),
    (1, 1, 1, 1, 4),
    (1, -1, 1, 1, 5),
    (-1, 1, 0, 1, 6),
    (-1, -1, 0, 1, 7),
    (0, 1, 0, 2, 8),
    (0, -1, 0, 2, 10),
)
SLOTS = 12
SOURCES = ((0, 1, 8, 9, 10, 11, 2, 4, 5), (0, 1, 8, 9, 10, 11, 3, 6, 7))
PLACES = ((4, 7, 3, 6, 5, 8, 1, 0, 2), (1, 4, 0, 3, 2, 5, 7, 6, 8))
GROUPS = (((), 0, 2), ((6, 7), 2, 6), ((0, 1, 2, 3, 4, 5), 6, 9))
GROUP_A, GROUP_B = 16, 32


def hops(step, size):
    return min(step, size - step)


STEPS_A = sorted(
    ((z, c) for z in range(8) for c in range(2) if z or c), key=lambda s: -2 * hops(s[0], 8) - s[1]
)
STEPS_B = sorted(
    ((y, x) for y in range(8) for x in range(4) if y or x), key=lambda s: -hops(s[0], 8) - hops(s[1], 4)
)


def window(z):
    return max(z - 1, 0), min(z + 2, DEPTH)


def kernel(
    offsets, start_hbm, blocks_hbm, moments_ref, last_ref,
    start, blocks, mats, buf, vecs, first, own, staged, landed, sums, turned, gather_a, gather_b,
    load_sem, send, recv, pair_send, pair_recv, a_send, a_recv, b_send, b_recv,
):
    gx, gy = lax.axis_index("gx"), lax.axis_index("gy")
    core = lax.rem(gx, 2)
    other = 1 - core
    chip = gx // 2
    half = lax.rem(core + chip + gy, 2)
    z_hi, col_x = gx // 8, lax.rem(gx, 8) // 2
    col_y, z_lo = gy // 4, lax.rem(gy, 4)
    in_a = (z_hi * 4 + z_lo) * 2 + core
    in_b = col_y * 4 + col_x

    def chip_at(dx, dy):
        return lax.rem(chip + dx + NX // 2, NX // 2), lax.rem(gy + dy + NY, NY)

    def neighbour(dx, dy):
        x, y = chip_at(dx, dy)
        return (2 * x + (core if (dx + dy) % 2 == 0 else other), y)

    def member_a(step):
        z, c = lax.rem(z_hi * 4 + z_lo + step[0], 8), lax.rem(core + step[1], 2)
        return z * 2 + c, ((z // 4) * 8 + col_x * 2 + c, col_y * 4 + lax.rem(z, 4))

    def member_b(step):
        y, x = lax.rem(col_y + step[0], 8), lax.rem(col_x + step[1], 4)
        return y * 4 + x, (z_hi * 8 + x * 2 + core, y * 4 + z_lo)

    load_vecs = pltpu.make_async_copy(start_hbm, start, load_sem.at[0])
    load_blocks = pltpu.make_async_copy(blocks_hbm, blocks, load_sem.at[1])
    load_vecs.start()
    load_blocks.start()

    barrier = pltpu.get_barrier_semaphore()

    def greet(device):
        pl.semaphore_signal(barrier, inc=1, device_id=device, device_id_type=MESH)

    for dx, dy, _, _, _ in MESSAGES:
        x, y = chip_at(dx, dy)
        for c in range(2):
            greet((2 * x + c, y))
    for step in STEPS_B:
        greet(member_b(step)[1])
    for step in STEPS_A:
        greet(member_a(step)[1])

    sums[...] = jnp.zeros_like(sums)
    load_vecs.wait()
    for ch in range(CHUNKS):
        for z in range(DEPTH):
            lanes = slice(z * TILE, (z + 1) * TILE)
            mine = pl.ds(pl.multiple_of(half * HALF + ch * ROWS, ROWS), ROWS)
            theirs = pl.ds(pl.multiple_of((1 - half) * HALF + ch * ROWS, ROWS), ROWS)
            first[core, ch, :, lanes] = start[z, mine, :]
            staged[ch, :, lanes] = start[z, theirs, :]
            for h in range(2):
                low = h * HALF + ch * ROWS
                own[h, ch, 0, :, lanes] = start[z, low : low + ROWS, :].astype(jnp.bfloat16)

    slots = lax.broadcasted_iota(jnp.int32, (DEPTH, CODES), 1)
    row_z = lax.broadcasted_iota(jnp.int32, (DEPTH, CODES), 0)
    codes = offsets[...]
    eye = jnp.where(
        lax.broadcasted_iota(jnp.int32, (TILE, TILE), 0) == lax.broadcasted_iota(jnp.int32, (TILE, TILE), 1), 1.0, 0.0
    ).astype(jnp.bfloat16)
    load_blocks.wait()
    for z in range(DEPTH):
        low, high = window(z)
        for i in range(9):
            place = jnp.where(core == 0, PLACES[0][i], PLACES[1][i])
            for w in range(high - low):
                code = place * 3 + low + w - z + 1
                pick = jnp.max(jnp.where((codes == code) & (row_z == z), slots, 0))
                block = lax.dot_general(
                    eye, blocks[z * CODES + pick], (((1,), (1,)), ((), ())), preferred_element_type=jnp.float32
                )
                at = (i * (high - low) + w) * TILE
                mats[core, z, at : at + TILE, :] = block.astype(jnp.bfloat16)

    pl.semaphore_wait(barrier, 2 * len(MESSAGES) + GROUP_A - 1 + GROUP_B - 1)

    side = 2 * core - 1
    first_sends = []
    for dx, dy, slot, receives, sends in (
        (side, 0, 3 - core, 1 - core, (0, 1)),
        (side, 1, 6 - 2 * core, 4 - 2 * core, (2, 3)),
        (side, -1, 7 - 2 * core, 5 - 2 * core, (4, 5)),
        (0, 1, 8 + core, 6, (6, 6)),
        (0, -1, 10 + core, 7, (7, 7)),
    ):
        x, y = chip_at(dx, dy)
        for c in range(2):
            first_sends.append((2 * x + c, y, lax.rem(c + x + y, 2), slot, receives, sends[c]))
    for ch in range(CHUNKS):
        for x, y, h, slot, receives, sends in first_sends:
            pltpu.make_async_remote_copy(
                src_ref=own.at[h, ch],
                dst_ref=buf.at[0, ch, pl.ds(slot, 1)],
                send_sem=send.at[0, ch, sends],
                recv_sem=recv.at[0, ch, receives],
                device_id=(x, y),
                device_id_type=MESH,
            ).start()

    partner = (2 * chip + other, gy)
    give_vecs = pltpu.make_async_remote_copy(
        src_ref=staged, dst_ref=first.at[core], send_sem=pair_send.at[0], recv_sem=pair_recv.at[0],
        device_id=partner, device_id_type=MESH,
    )
    give_vecs.start()
    give_mats = pltpu.make_async_remote_copy(
        src_ref=mats.at[core], dst_ref=mats.at[core], send_sem=pair_send.at[1], recv_sem=pair_recv.at[1],
        device_id=partner, device_id_type=MESH,
    )

    def copies(p, ch):
        return [
            pltpu.make_async_remote_copy(
                src_ref=buf.at[p, ch, lo : lo + count],
                dst_ref=buf.at[p, ch, slot : slot + count],
                send_sem=send.at[p, ch, i],
                recv_sem=recv.at[p, ch, i],
                device_id=neighbour(dx, dy),
                device_id_type=MESH,
            )
            for i, (dx, dy, lo, count, slot) in enumerate(MESSAGES)
        ]

    def fold(value):
        return sum(value[:, z * TILE : (z + 1) * TILE] for z in range(DEPTH))

    def row_of_sums(i, count):
        return jnp.sum(jnp.transpose(turned[i, :count]), axis=0, keepdims=True)

    give_mats.start()
    give_vecs.wait_recv()
    for ch in range(CHUNKS):
        total = jnp.zeros((ROWS, TILE), jnp.float32)
        for a in range(2):
            value = first[a, ch]
            buf[0, ch, a] = value.astype(jnp.bfloat16)
            vecs[0, a, ch] = value
            total = total + fold(value * value)
        turned[0, ch * ROWS : (ch + 1) * ROWS, :] = total
    give_mats.wait_recv()

    def products(p, ch, a, group, accs):
        _, begin, end = GROUPS[group]
        pieces = [buf[p, ch, SOURCES[a][i]] for i in range(begin, end)]
        for z in range(DEPTH):
            low, high = window(z)
            wide = (high - low) * TILE
            left = jnp.concatenate([piece[:, low * TILE : high * TILE] for piece in pieces], axis=1)
            part = jnp.dot(left, mats[a, z, begin * wide : end * wide, :], preferred_element_type=jnp.float32)
            accs[z] = part if accs[z] is None else accs[z] + part

    def step(n, p, is_first, is_last):
        q = 1 - p
        for ch in range(CHUNKS):
            accs = [[None] * DEPTH for _ in range(2)]
            arriving = copies(p, ch)
            for group in range(2):
                for i in GROUPS[group][0]:
                    arriving[i].wait_recv()
                for a in range(2):
                    products(p, ch, a, group, accs[a])
            if not is_first:
                for copy in copies(q, ch):
                    copy.wait_send()
            for i in GROUPS[2][0]:
                arriving[i].wait_recv()
            for a in range(2):
                products(p, ch, a, 2, accs[a])
            for a in range(2):
                for z in range(DEPTH):
                    lanes = slice(z * TILE, (z + 1) * TILE)
                    value = accs[a][z] if is_first else 2.0 * accs[a][z] - vecs[q, a, ch, :, lanes]
                    vecs[q, a, ch, :, lanes] = value
                    if not is_last:
                        buf[q, ch, a, :, lanes] = value.astype(jnp.bfloat16)
            if not is_last:
                for copy in copies(q, ch):
                    copy.start()
            total = sum(fold(vecs[q, a, ch] * first[a, ch]) for a in range(2))
            at = lax.rem(n + 1, 4) * HALF + ch * ROWS
            turned[(n + 1) // 4, pl.ds(pl.multiple_of(at, ROWS), ROWS), :] = total

    def middle(n, carry):
        step(n, lax.rem(n, 2), False, False)
        return carry

    step(jnp.int32(0), 0, True, False)
    lax.fori_loop(1, STEPS - 1, middle, 0)
    for i in range(2):
        sums[0, :, i * TILE : (i + 1) * TILE] = row_of_sums(i, TILE)
    step(jnp.int32(STEPS - 1), (STEPS - 1) % 2, False, True)

    final = STEPS % 2
    give_last = pltpu.make_async_remote_copy(
        src_ref=vecs.at[final, other], dst_ref=landed, send_sem=pair_send.at[2], recv_sem=pair_recv.at[2],
        device_id=partner, device_id_type=MESH,
    )
    give_last.start()

    sums[0, :, 2 * TILE : 2 * TILE + HALF] = row_of_sums(2, HALF)

    def share(source, gathered, me, member, steps, sent, received, meanwhile):
        partners = [member(step) for step in steps]

        def copy(i, slot):
            return pltpu.make_async_remote_copy(
                src_ref=source, dst_ref=gathered.at[slot], send_sem=sent.at[i], recv_sem=received.at[slot],
                device_id=partners[i][1], device_id_type=MESH,
            )

        for i in range(len(steps)):
            copy(i, me).start()
        gathered[me] = source[...]
        meanwhile()
        for i in range(len(steps)):
            copy(i, me).wait_send()
        for i, (who, _) in enumerate(partners):
            copy(i, who).wait_recv()
        return jnp.sum(gathered[...], axis=0)

    def assemble():
        for ch in range(CHUNKS):
            for z in range(DEPTH):
                lanes = slice(z * TILE, (z + 1) * TILE)
                mine = pl.ds(pl.multiple_of(half * HALF + ch * ROWS, ROWS), ROWS)
                last_ref[z, mine, :] = vecs[final, core, ch, :, lanes]
        for copy in (give_vecs, give_mats):
            copy.wait_send()
        for ch in range(CHUNKS):
            for copy in copies((STEPS - 1) % 2, ch):
                copy.wait_send()

    def assemble_rest():
        give_last.wait_recv()
        for ch in range(CHUNKS):
            for z in range(DEPTH):
                lanes = slice(z * TILE, (z + 1) * TILE)
                theirs = pl.ds(pl.multiple_of((1 - half) * HALF + ch * ROWS, ROWS), ROWS)
                last_ref[z, theirs, :] = landed[ch, :, lanes]
        give_last.wait_send()

    sums[1] = share(sums.at[0], gather_a, in_a, member_a, STEPS_A, a_send, a_recv, assemble)
    result_b = share(sums.at[1], gather_b, in_b, member_b, STEPS_B, b_send, b_recv, assemble_rest)
    scaled = result_b * (1.0 / (NX * NY * DEPTH * TILE))
    for n in range(STEPS + 1):
        row = jnp.broadcast_to(scaled[:, n // 4 * TILE : (n // 4 + 1) * TILE], (8, TILE))
        if n % 4:
            row = pltpu.roll(row, TILE - n % 4 * HALF, 1)
        moments_ref[n : n + 1, :] = row[0:1, :HALF]


def body(start_vecs, force_blocks, slot_offsets):
    vec_shape = (2, CHUNKS, ROWS, WIDE)
    count = len(MESSAGES)
    moments, last = pl.pallas_call(
        kernel,
        out_shape=(
            jax.ShapeDtypeStruct((STEPS + 1, HALF), jnp.float32),
            jax.ShapeDtypeStruct((DEPTH, 2 * HALF, TILE), jnp.float32),
        ),
        in_specs=[
            pl.BlockSpec(memory_space=pltpu.VMEM),
            pl.BlockSpec(memory_space=pltpu.HBM),
            pl.BlockSpec(memory_space=pltpu.HBM),
        ],
        out_specs=(pl.BlockSpec(memory_space=pltpu.VMEM), pl.BlockSpec(memory_space=pltpu.VMEM)),
        scratch_shapes=[
            pltpu.VMEM((DEPTH, 2 * HALF, TILE), jnp.float32),
            pltpu.VMEM((DEPTH * CODES, TILE, TILE), jnp.bfloat16),
            pltpu.VMEM((2, DEPTH, 27 * TILE, TILE), jnp.bfloat16),
            pltpu.VMEM((2, CHUNKS, SLOTS, ROWS, WIDE), jnp.bfloat16),
            pltpu.VMEM((2,) + vec_shape, jnp.float32),
            pltpu.VMEM(vec_shape, jnp.float32),
            pltpu.VMEM((2, CHUNKS, 1, ROWS, WIDE), jnp.bfloat16),
            pltpu.VMEM(vec_shape[1:], jnp.float32),
            pltpu.VMEM(vec_shape[1:], jnp.float32),
            pltpu.VMEM((2, 1, 3 * TILE), jnp.float32),
            pltpu.VMEM((3, TILE, TILE), jnp.float32),
            pltpu.VMEM((GROUP_A, 1, 3 * TILE), jnp.float32),
            pltpu.VMEM((GROUP_B, 1, 3 * TILE), jnp.float32),
            pltpu.SemaphoreType.DMA((2,)),
            pltpu.SemaphoreType.DMA((2, CHUNKS, count)),
            pltpu.SemaphoreType.DMA((2, CHUNKS, count)),
            pltpu.SemaphoreType.DMA((3,)),
            pltpu.SemaphoreType.DMA((3,)),
            pltpu.SemaphoreType.DMA((GROUP_A,)),
            pltpu.SemaphoreType.DMA((GROUP_A,)),
            pltpu.SemaphoreType.DMA((GROUP_B,)),
            pltpu.SemaphoreType.DMA((GROUP_B,)),
        ],
        compiler_params=pltpu.CompilerParams(
            collective_id=0, has_side_effects=True, vmem_limit_bytes=55008 << 10
        ),
    )(
        slot_offsets.reshape(DEPTH, CODES),
        start_vecs.reshape(DEPTH, 2 * HALF, TILE),
        force_blocks.reshape(DEPTH * CODES, TILE, TILE),
    )
    return moments, last.reshape(1, 1, DEPTH, 2 * HALF, TILE)


def solution(mesh):
    in_specs = (
        P("gx", "gy", None, None, None),
        P("gx", "gy", None, None, None, None),
        P("gx", "gy", None, None),
    )
    out_specs = (P(), P("gx", "gy", None, None, None))
    return jax.shard_map(body, mesh=mesh, in_specs=in_specs, out_specs=out_specs, check_vma=False)
```

```python
import jax
import jax.numpy as jnp
from jax import lax
from jax.experimental import pallas as pl
from jax.experimental.pallas import tpu as pltpu
from jax.sharding import PartitionSpec as P

STEPS = 8
TILE = 128
DEPTH = 4
CODES = 27
CHUNKS = 2
HALF = 32
ROWS = HALF // CHUNKS
WIDE = DEPTH * TILE
NX, NY = 16, 32
MESH = pl.DeviceIdType.MESH

MESSAGES = (
    (1, 0, 1, 1, 2),
    (-1, 0, 0, 1, 3),
    (1, 1, 1, 1, 4),
    (1, -1, 1, 1, 5),
    (-1, 1, 0, 1, 6),
    (-1, -1, 0, 1, 7),
    (0, 1, 0, 2, 8),
    (0, -1, 0, 2, 10),
)
SLOTS = 12
SOURCES = ((0, 1, 8, 9, 10, 11, 2, 4, 5), (0, 1, 8, 9, 10, 11, 3, 6, 7))
PLACES = ((4, 7, 3, 6, 5, 8, 1, 0, 2), (1, 4, 0, 3, 2, 5, 7, 6, 8))
GROUPS = (((), 0, 2), ((6, 7), 2, 6), ((0, 1, 2, 3, 4, 5), 6, 9))
LEAVING = ((1, 4, 5, 6, 7), (0, 2, 3))
GROUP_A, GROUP_B = 16, 32


def hops(step, size):
    return min(step, size - step)


STEPS_A = sorted(
    ((z, c) for z in range(8) for c in range(2) if z or c), key=lambda s: -2 * hops(s[0], 8) - s[1]
)
STEPS_B = sorted(
    ((y, x) for y in range(8) for x in range(4) if y or x), key=lambda s: -hops(s[0], 8) - hops(s[1], 4)
)


def window(z):
    return max(z - 1, 0), min(z + 2, DEPTH)


def kernel(
    offsets, start_hbm, blocks_hbm, moments_ref, last_ref,
    start, blocks, mats, buf, vecs, first, own, staged, landed, early, late, turned, early_a, early_b, late_a, late_b,
    load_sem, send, recv, pair_send, pair_recv, a_send, a_recv, b_send, b_recv,
):
    gx, gy = lax.axis_index("gx"), lax.axis_index("gy")
    core = lax.rem(gx, 2)
    other = 1 - core
    chip = gx // 2
    half = lax.rem(core + chip + gy, 2)
    z_hi, col_x = gx // 8, lax.rem(gx, 8) // 2
    col_y, z_lo = gy // 4, lax.rem(gy, 4)
    in_a = (z_hi * 4 + z_lo) * 2 + core
    in_b = col_y * 4 + col_x

    def chip_at(dx, dy):
        return lax.rem(chip + dx + NX // 2, NX // 2), lax.rem(gy + dy + NY, NY)

    def neighbour(dx, dy):
        x, y = chip_at(dx, dy)
        return (2 * x + (core if (dx + dy) % 2 == 0 else other), y)

    def member_a(step):
        z, c = lax.rem(z_hi * 4 + z_lo + step[0], 8), lax.rem(core + step[1], 2)
        return z * 2 + c, ((z // 4) * 8 + col_x * 2 + c, col_y * 4 + lax.rem(z, 4))

    def member_b(step):
        y, x = lax.rem(col_y + step[0], 8), lax.rem(col_x + step[1], 4)
        return y * 4 + x, (z_hi * 8 + x * 2 + core, y * 4 + z_lo)

    load_vecs = pltpu.make_async_copy(start_hbm, start, load_sem.at[0])
    load_blocks = pltpu.make_async_copy(blocks_hbm, blocks, load_sem.at[1])
    load_vecs.start()
    load_blocks.start()

    barrier = pltpu.get_barrier_semaphore()

    def greet(device):
        pl.semaphore_signal(barrier, inc=1, device_id=device, device_id_type=MESH)

    for dx, dy, _, _, _ in MESSAGES:
        x, y = chip_at(dx, dy)
        for c in range(2):
            greet((2 * x + c, y))
    for step in STEPS_B:
        greet(member_b(step)[1])
    for step in STEPS_A:
        greet(member_a(step)[1])

    turned[...] = jnp.zeros_like(turned)
    load_vecs.wait()
    for ch in range(CHUNKS):
        for z in range(DEPTH):
            lanes = slice(z * TILE, (z + 1) * TILE)
            mine = pl.ds(pl.multiple_of(half * HALF + ch * ROWS, ROWS), ROWS)
            theirs = pl.ds(pl.multiple_of((1 - half) * HALF + ch * ROWS, ROWS), ROWS)
            first[core, ch, :, lanes] = start[z, mine, :]
            staged[ch, :, lanes] = start[z, theirs, :]
            for h in range(2):
                low = h * HALF + ch * ROWS
                own[h, ch, 0, :, lanes] = start[z, low : low + ROWS, :].astype(jnp.bfloat16)

    slots = lax.broadcasted_iota(jnp.int32, (DEPTH, CODES), 1)
    row_z = lax.broadcasted_iota(jnp.int32, (DEPTH, CODES), 0)
    codes = offsets[...]
    eye = jnp.where(
        lax.broadcasted_iota(jnp.int32, (TILE, TILE), 0) == lax.broadcasted_iota(jnp.int32, (TILE, TILE), 1), 1.0, 0.0
    ).astype(jnp.bfloat16)
    load_blocks.wait()
    for z in range(DEPTH):
        low, high = window(z)
        for i in range(9):
            place = jnp.where(core == 0, PLACES[0][i], PLACES[1][i])
            for w in range(high - low):
                code = place * 3 + low + w - z + 1
                pick = jnp.max(jnp.where((codes == code) & (row_z == z), slots, 0))
                block = lax.dot_general(
                    eye, blocks[z * CODES + pick], (((1,), (1,)), ((), ())), preferred_element_type=jnp.float32
                )
                at = (i * (high - low) + w) * TILE
                mats[core, z, at : at + TILE, :] = block.astype(jnp.bfloat16)

    pl.semaphore_wait(barrier, 2 * len(MESSAGES) + GROUP_A - 1 + GROUP_B - 1)

    side = 2 * core - 1
    first_sends = []
    for dx, dy, slot, receives, sends in (
        (side, 0, 3 - core, 1 - core, (0, 1)),
        (side, 1, 6 - 2 * core, 4 - 2 * core, (2, 3)),
        (side, -1, 7 - 2 * core, 5 - 2 * core, (4, 5)),
        (0, 1, 8 + core, 6, (6, 6)),
        (0, -1, 10 + core, 7, (7, 7)),
    ):
        x, y = chip_at(dx, dy)
        for c in range(2):
            first_sends.append((2 * x + c, y, lax.rem(c + x + y, 2), slot, receives, sends[c]))
    for ch in range(CHUNKS):
        for x, y, h, slot, receives, sends in first_sends:
            pltpu.make_async_remote_copy(
                src_ref=own.at[h, ch],
                dst_ref=buf.at[0, ch, pl.ds(slot, 1)],
                send_sem=send.at[0, ch, sends],
                recv_sem=recv.at[0, ch, receives],
                device_id=(x, y),
                device_id_type=MESH,
            ).start()

    partner = (2 * chip + other, gy)
    give_vecs = pltpu.make_async_remote_copy(
        src_ref=staged, dst_ref=first.at[core], send_sem=pair_send.at[0], recv_sem=pair_recv.at[0],
        device_id=partner, device_id_type=MESH,
    )
    give_vecs.start()
    give_mats = pltpu.make_async_remote_copy(
        src_ref=mats.at[core], dst_ref=mats.at[core], send_sem=pair_send.at[1], recv_sem=pair_recv.at[1],
        device_id=partner, device_id_type=MESH,
    )

    def copies(p, ch):
        return [
            pltpu.make_async_remote_copy(
                src_ref=buf.at[p, ch, lo : lo + count],
                dst_ref=buf.at[p, ch, slot : slot + count],
                send_sem=send.at[p, ch, i],
                recv_sem=recv.at[p, ch, i],
                device_id=neighbour(dx, dy),
                device_id_type=MESH,
            )
            for i, (dx, dy, lo, count, slot) in enumerate(MESSAGES)
        ]

    def fold(value):
        return sum(value[:, z * TILE : (z + 1) * TILE] for z in range(DEPTH))

    def row_of_sums(i):
        return jnp.sum(jnp.transpose(turned[i]), axis=0, keepdims=True)

    give_mats.start()
    give_vecs.wait_recv()
    for ch in range(CHUNKS):
        total = jnp.zeros((ROWS, TILE), jnp.float32)
        for a in range(2):
            value = first[a, ch]
            buf[0, ch, a] = value.astype(jnp.bfloat16)
            vecs[0, a, ch] = value
            total = total + fold(value * value)
        turned[0, ch * ROWS : (ch + 1) * ROWS, :] = total
    give_mats.wait_recv()

    def products(p, ch, a, group, accs):
        _, begin, end = GROUPS[group]
        pieces = [buf[p, ch, SOURCES[a][i]] for i in range(begin, end)]
        for z in range(DEPTH):
            low, high = window(z)
            wide = (high - low) * TILE
            left = jnp.concatenate([piece[:, low * TILE : high * TILE] for piece in pieces], axis=1)
            part = jnp.dot(left, mats[a, z, begin * wide : end * wide, :], preferred_element_type=jnp.float32)
            accs[z] = part if accs[z] is None else accs[z] + part

    def share(k, source, gathered, me, member, steps, sent, received):
        partners = [member(step) for step in steps]

        def copy(i, slot):
            return pltpu.make_async_remote_copy(
                src_ref=source, dst_ref=gathered.at[slot], send_sem=sent.at[k, i], recv_sem=received.at[k, slot],
                device_id=partners[i][1], device_id_type=MESH,
            )

        for i in range(len(steps)):
            copy(i, me).start()
        gathered[me] = source[...]

        def finish():
            for i in range(len(steps)):
                copy(i, me).wait_send()
            for i, (who, _) in enumerate(partners):
                copy(i, who).wait_recv()
            return jnp.sum(gathered[...], axis=0)

        return finish

    def step(n, p, is_first, is_last, between=None):
        q = 1 - p
        for ch in range(CHUNKS):
            accs = [[None] * DEPTH for _ in range(2)]
            arriving = copies(p, ch)
            for group in range(2):
                for i in GROUPS[group][0]:
                    arriving[i].wait_recv()
                for a in range(2):
                    products(p, ch, a, group, accs[a])
            if not is_first:
                for copy in copies(q, ch):
                    copy.wait_send()
            for i in GROUPS[2][0]:
                arriving[i].wait_recv()
            leaving = copies(q, ch)
            for a in (1, 0):
                products(p, ch, a, 2, accs[a])
                for z in range(DEPTH):
                    lanes = slice(z * TILE, (z + 1) * TILE)
                    value = accs[a][z] if is_first else 2.0 * accs[a][z] - vecs[q, a, ch, :, lanes]
                    vecs[q, a, ch, :, lanes] = value
                    if not is_last:
                        buf[q, ch, a, :, lanes] = value.astype(jnp.bfloat16)
                if not is_last:
                    for i in LEAVING[a]:
                        leaving[i].start()
            total = sum(fold(vecs[q, a, ch] * first[a, ch]) for a in range(2))
            at = lax.rem(n + 1, 4) * HALF + ch * ROWS
            turned[(n + 1) // 4, pl.ds(pl.multiple_of(at, ROWS), ROWS), :] = total
            if between is not None and ch == 0:
                between()

    def middle(n, carry):
        step(n, lax.rem(n, 2), False, False)
        return carry

    step(jnp.int32(0), 0, True, False)
    lax.fori_loop(1, STEPS - 1, middle, 0)
    for i in range(2):
        early[0, :, i * TILE : (i + 1) * TILE] = row_of_sums(i)
    finish_early_a = share(0, early.at[0], early_a, in_a, member_a, STEPS_A, a_send, a_recv)
    finish_early = []

    def between():
        early[1] = finish_early_a()
        finish_early.append(share(0, early.at[1], early_b, in_b, member_b, STEPS_B, b_send, b_recv))

    step(jnp.int32(STEPS - 1), (STEPS - 1) % 2, False, True, between)

    final = STEPS % 2
    give_last = pltpu.make_async_remote_copy(
        src_ref=vecs.at[final, other], dst_ref=landed, send_sem=pair_send.at[2], recv_sem=pair_recv.at[2],
        device_id=partner, device_id_type=MESH,
    )
    give_last.start()

    late[0] = row_of_sums(2)

    def assemble():
        for ch in range(CHUNKS):
            for z in range(DEPTH):
                lanes = slice(z * TILE, (z + 1) * TILE)
                mine = pl.ds(pl.multiple_of(half * HALF + ch * ROWS, ROWS), ROWS)
                last_ref[z, mine, :] = vecs[final, core, ch, :, lanes]
        for copy in (give_vecs, give_mats):
            copy.wait_send()
        for ch in range(CHUNKS):
            for copy in copies((STEPS - 1) % 2, ch):
                copy.wait_send()

    def assemble_rest():
        give_last.wait_recv()
        for ch in range(CHUNKS):
            for z in range(DEPTH):
                lanes = slice(z * TILE, (z + 1) * TILE)
                theirs = pl.ds(pl.multiple_of((1 - half) * HALF + ch * ROWS, ROWS), ROWS)
                last_ref[z, theirs, :] = landed[ch, :, lanes]
        give_last.wait_send()

    finish_late_a = share(1, late.at[0], late_a, in_a, member_a, STEPS_A, a_send, a_recv)
    assemble()
    late[1] = finish_late_a()
    finish_late_b = share(1, late.at[1], late_b, in_b, member_b, STEPS_B, b_send, b_recv)
    assemble_rest()
    result_b = jnp.concatenate([finish_early[0](), finish_late_b()], axis=1)
    scaled = result_b * (1.0 / (NX * NY * DEPTH * TILE))
    for n in range(STEPS + 1):
        row = jnp.broadcast_to(scaled[:, n // 4 * TILE : (n // 4 + 1) * TILE], (8, TILE))
        if n % 4:
            row = pltpu.roll(row, TILE - n % 4 * HALF, 1)
        moments_ref[n : n + 1, :] = row[0:1, :HALF]


def body(start_vecs, force_blocks, slot_offsets):
    vec_shape = (2, CHUNKS, ROWS, WIDE)
    count = len(MESSAGES)
    moments, last = pl.pallas_call(
        kernel,
        out_shape=(
            jax.ShapeDtypeStruct((STEPS + 1, HALF), jnp.float32),
            jax.ShapeDtypeStruct((DEPTH, 2 * HALF, TILE), jnp.float32),
        ),
        in_specs=[
            pl.BlockSpec(memory_space=pltpu.VMEM),
            pl.BlockSpec(memory_space=pltpu.HBM),
            pl.BlockSpec(memory_space=pltpu.HBM),
        ],
        out_specs=(pl.BlockSpec(memory_space=pltpu.VMEM), pl.BlockSpec(memory_space=pltpu.VMEM)),
        scratch_shapes=[
            pltpu.VMEM((DEPTH, 2 * HALF, TILE), jnp.float32),
            pltpu.VMEM((DEPTH * CODES, TILE, TILE), jnp.bfloat16),
            pltpu.VMEM((2, DEPTH, 27 * TILE, TILE), jnp.bfloat16),
            pltpu.VMEM((2, CHUNKS, SLOTS, ROWS, WIDE), jnp.bfloat16),
            pltpu.VMEM((2,) + vec_shape, jnp.float32),
            pltpu.VMEM(vec_shape, jnp.float32),
            pltpu.VMEM((2, CHUNKS, 1, ROWS, WIDE), jnp.bfloat16),
            pltpu.VMEM(vec_shape[1:], jnp.float32),
            pltpu.VMEM(vec_shape[1:], jnp.float32),
            pltpu.VMEM((2, 1, 2 * TILE), jnp.float32),
            pltpu.VMEM((2, 1, TILE), jnp.float32),
            pltpu.VMEM((3, TILE, TILE), jnp.float32),
            pltpu.VMEM((GROUP_A, 1, 2 * TILE), jnp.float32),
            pltpu.VMEM((GROUP_B, 1, 2 * TILE), jnp.float32),
            pltpu.VMEM((GROUP_A, 1, TILE), jnp.float32),
            pltpu.VMEM((GROUP_B, 1, TILE), jnp.float32),
            pltpu.SemaphoreType.DMA((2,)),
            pltpu.SemaphoreType.DMA((2, CHUNKS, count)),
            pltpu.SemaphoreType.DMA((2, CHUNKS, count)),
            pltpu.SemaphoreType.DMA((3,)),
            pltpu.SemaphoreType.DMA((3,)),
            pltpu.SemaphoreType.DMA((2, GROUP_A)),
            pltpu.SemaphoreType.DMA((2, GROUP_A)),
            pltpu.SemaphoreType.DMA((2, GROUP_B)),
            pltpu.SemaphoreType.DMA((2, GROUP_B)),
        ],
        compiler_params=pltpu.CompilerParams(
            collective_id=0, has_side_effects=True, vmem_limit_bytes=55008 << 10
        ),
    )(
        slot_offsets.reshape(DEPTH, CODES),
        start_vecs.reshape(DEPTH, 2 * HALF, TILE),
        force_blocks.reshape(DEPTH * CODES, TILE, TILE),
    )
    return moments, last.reshape(1, 1, DEPTH, 2 * HALF, TILE)


def solution(mesh):
    in_specs = (
        P("gx", "gy", None, None, None),
        P("gx", "gy", None, None, None, None),
        P("gx", "gy", None, None),
    )
    out_specs = (P(), P("gx", "gy", None, None, None))
    return jax.shard_map(body, mesh=mesh, in_specs=in_specs, out_specs=out_specs, check_vma=False)
```
